32 devices in a mesh: dp: 16 (over z, y, x), tensor: 2 (over core).
Axes of the slice: x: 2, y: 2, z: 4, core: 2. Of those that a mesh axis runs over, the one named last changes fastest.
Arguments:
- tokens_in: bfloat16 [16, 1024, 1024], P('dp', 'tensor'), may hold values from -6 to 6
- segments: int32 [16, 1024], P('dp'), may hold values from 0 to 4, as said below
- gains: bfloat16 [4, 1024], P(None, 'dp'), may hold values from 0.5 to 1.5
- taps: bfloat16 [3, 1024], P(None, 'dp'), may hold values from -3 to 3
- in_proj: bfloat16 [1024, 3, 1024], P('dp', None, 'tensor'), may hold values from -0.1875 to 0.1875
- out_proj: bfloat16 [1024, 1024], P('tensor', 'dp'), may hold values from -0.1875 to 0.1875
- gate_up_a: bfloat16 [1024, 2, 4608], P('dp', None, 'tensor'), may hold values from -0.1875 to 0.1875
- down_a: bfloat16 [4608, 1024], P('tensor', 'dp'), may hold values from -0.09375 to 0.09375
- query_w: bfloat16 [1024, 1024], P('dp', 'tensor'), may hold values from -0.1875 to 0.1875
- key_value_w: bfloat16 [1024, 2, 512], P('dp', None, 'tensor'), may hold values from -0.1875 to 0.1875
- attn_out_w: bfloat16 [1024, 1024], P('tensor', 'dp'), may hold values from -0.75 to 0.75
- gate_up_b: bfloat16 [1024, 2, 4608], P('dp', None, 'tensor'), may hold values from -0.1875 to 0.1875
- down_b: bfloat16 [4608, 1024], P('tensor', 'dp'), may hold values from -0.09375 to 0.09375
- cotangent: bfloat16 [16, 1024, 1024], P('dp', 'tensor'), may hold values from -6 to 6
Outputs:
- output: bfloat16 [16, 1024, 1024], P('dp', 'tensor')
- grad_input: float32 [16, 1024, 1024], P('dp', 'tensor')
- grad_gains: float32 [4, 1024], P(None, 'dp')
- grad_taps: float32 [3, 1024], P(None, 'dp')
- grad_in_proj: float32 [1024, 3, 1024], P('dp', None, 'tensor')
- grad_out_proj: float32 [1024, 1024], P('tensor', 'dp')
- grad_gate_up_a: float32 [1024, 2, 4608], P('dp', None, 'tensor')
- grad_down_a: float32 [4608, 1024], P('tensor', 'dp')
- grad_query: float32 [1024, 1024], P('dp', 'tensor')
- grad_key_value: float32 [1024, 2, 512], P('dp', None, 'tensor')
- grad_attn_out: float32 [1024, 1024], P('tensor', 'dp')
- grad_gate_up_b: float32 [1024, 2, 4608], P('dp', None, 'tensor')
- grad_down_b: float32 [4608, 1024], P('tensor', 'dp')
The draws below stay inside these ranges and needn't reach their ends.
Inputs may be any that keep to these rules, and one draw needn't show every extreme that they name: `segments`: along each sequence the numbers start at 0, never fall, and rise by at most 1 from one token to the next; the last token's number is 4 (each sequence holds exactly 5 documents); the document that holds token 512 holds all tokens from 384 to 639.
All inputs are finite; a program needn't handle non-finite values.
Results may differ from the reference program's by a relative error of at most 0.03.
Values may be sent and summed in bfloat16 or wider, within the bound.
No kernel may reach another device: no remote copies, remote signals or barrier semaphores. Data moves between devices by JAX's collectives and lax.ppermute only.
A program may use at most 320 MiB of HBM per device.

```python
import math
import jax
import jax.numpy as jnp
import numpy as np
from jax import lax

D = 1024
FF = 4608
H = 16
KV = 8
HD = 64
SEQ = 1024
NSEQ = 16


def draw_segments(key, part):
    key = jax.random.fold_in(key, 11)
    cut_count = max(2, SEQ // 256)
    middle = SEQ // 2
    reach = SEQ // 8
    places = np.arange(1, SEQ)
    places = places[np.abs(places - middle) >= reach].astype(np.int32)
    allowed_places = jnp.asarray(places)
    row_keys = jax.random.split(key, NSEQ)
    picked = jax.vmap(lambda row_key: jax.random.permutation(row_key, allowed_places)[:cut_count])(row_keys)
    marks = jnp.zeros((NSEQ, SEQ), jnp.int32).at[jnp.arange(NSEQ)[:, None], picked].set(1)
    return jnp.cumsum(marks, axis=1).astype(jnp.int32)


def block_levels(stream_key, extent, cuts, least, top_value):
    loudness = 1.0
    for axis_at, blocks in cuts:
        steps = jax.random.uniform(jax.random.fold_in(jax.random.fold_in(stream_key, 6), axis_at), (blocks,), jnp.float32, least / len(cuts), top_value / len(cuts))
        loudness = loudness * jnp.repeat(jnp.exp(steps), extent[axis_at] // blocks).reshape((-1,) + (1,) * (len(extent) - 1 - axis_at))
    return loudness


def centred(stream_key, dims, width, bound, shards=(), held_as=jnp.bfloat16):
    level = block_levels(stream_key, dims, shards, -0.22, 0.18) if shards else 1.0
    result = jax.random.normal(stream_key, dims, jnp.float32) * width * level
    return jnp.minimum(jnp.maximum(result, -bound), bound).astype(held_as)


def setup_inputs(seed: int = 0) -> dict:
    splits = jax.random.split(jax.random.key(seed), 15)
    tokens_in = centred(splits[0], (NSEQ, SEQ, D), 1.0, 6.0, ((0, 16), (1, 2)))
    segments = draw_segments(jax.random.fold_in(splits[14], 71), 0)
    gains = jnp.clip(1.0 + 0.1 * jax.random.normal(splits[2], (4, D), jnp.float32), 0.5, 1.5).astype(jnp.bfloat16)
    taps = centred(splits[3], (3, D), 0.5, 3.0, ((1, 16),))
    in_proj = centred(splits[4], (D, 3, D), D ** -0.5, 0.1875, ((0, 16), (2, 2)))
    out_proj = centred(splits[5], (D, D), D ** -0.5, 0.1875, ((0, 2), (1, 16)))
    gate_up_a = centred(splits[6], (D, 2, FF), D ** -0.5, 0.1875, ((0, 16), (2, 2)))
    down_a = centred(splits[7], (FF, D), FF ** -0.5, 0.09375, ((0, 2), (1, 16)))
    query_w = centred(splits[8], (D, H * HD), D ** -0.5, 0.1875, ((0, 16), (1, 2)))
    key_value_w = centred(splits[9], (D, 2, KV * HD), D ** -0.5, 0.1875, ((0, 16), (2, 2)))
    attn_out_w = centred(splits[10], (H * HD, D), (H * HD // 16) ** -0.5, 0.75, ((0, 2), (1, 16)))
    gate_up_b = centred(splits[11], (D, 2, FF), D ** -0.5, 0.1875, ((0, 16), (2, 2)))
    down_b = centred(splits[12], (FF, D), FF ** -0.5, 0.09375, ((0, 2), (1, 16)))
    cotangent = centred(splits[13], (NSEQ, SEQ, D), 1.0, 6.0, ((0, 16), (1, 2)))
    return dict(tokens_in=tokens_in, segments=segments, gains=gains, taps=taps, in_proj=in_proj, out_proj=out_proj, gate_up_a=gate_up_a, down_a=down_a, query_w=query_w, key_value_w=key_value_w, attn_out_w=attn_out_w, gate_up_b=gate_up_b, down_b=down_b, cotangent=cotangent)


EPS = 1e-05
THETA = 1000000.0
SCALE = 0.125

@jax.custom_vjp
def low(v):
    return lax.optimization_barrier(v.astype(jnp.bfloat16)).astype(jnp.float32)

@jax.custom_vjp
def low_back(v):
    return v

def low_keep(v):
    return (low(v), None)

def low_pass(kept, grad):
    return (grad,)

def back_keep(v):
    return (v, None)

def back_low(kept, grad):
    return (low(grad),)
low.defvjp(low_keep, low_pass)
low_back.defvjp(back_keep, back_low)

def matmul(left, right):
    return jnp.dot(left, right, precision=lax.Precision.HIGHEST)

def contract(form, left, right):
    return jnp.einsum(form, left, right, precision=lax.Precision.HIGHEST)

def norm_rows(values_in, gain):
    return values_in * lax.rsqrt(lax.optimization_barrier(jnp.mean(values_in * values_in, axis=-1, keepdims=True)) + EPS) * gain

def doc_positions(segment_ids):
    length = segment_ids.shape[0]
    index = jnp.arange(length, dtype=jnp.int32)
    starts = jnp.concatenate([jnp.ones((1,), jnp.bool_), segment_ids[1:] != segment_ids[:-1]])
    first = lax.cummax(jnp.where(starts, index, 0), axis=0)
    return (index - first).astype(jnp.float32)

def rope(values_in, positions):
    half = values_in.shape[-1] // 2
    freq = jnp.exp(jnp.arange(half, dtype=jnp.float32) * (-2.0 * math.log(THETA) / (2 * half)))
    angle = positions[:, None] * freq[None, :]
    cosine = jnp.cos(angle)[:, None, :]
    sine = jnp.sin(angle)[:, None, :]
    first_half = values_in[..., :half]
    second_half = values_in[..., half:]
    return jnp.concatenate([first_half * cosine - second_half * sine, second_half * cosine + first_half * sine], axis=-1)

def conv_mix(mixed, kernel, segment_ids):
    driven = mixed[:, 0] * mixed[:, 2]
    channels = driven.shape[1]
    same_one = jnp.concatenate([jnp.zeros((1,), jnp.bool_), segment_ids[1:] == segment_ids[:-1]]).astype(driven.dtype)
    same_two = jnp.concatenate([jnp.zeros((2,), jnp.bool_), segment_ids[2:] == segment_ids[:-2]]).astype(driven.dtype)
    back_one = jnp.concatenate([jnp.zeros((1, channels), driven.dtype), driven[:-1]], axis=0) * same_one[:, None]
    back_two = jnp.concatenate([jnp.zeros((2, channels), driven.dtype), driven[:-2]], axis=0) * same_two[:, None]
    return mixed[:, 1] * (kernel[0] * driven + kernel[1] * back_one + kernel[2] * back_two)

def glu(gate_up):
    return jax.nn.silu(gate_up[:, 0]) * gate_up[:, 1]

def attention_core(query, keys, values, segment_ids):
    length = query.shape[0]
    index = jnp.arange(length)
    allowed = (index[None, :] <= index[:, None]) & (segment_ids[None, :] == segment_ids[:, None])
    scores = low_back(SCALE * contract('qhgd,khd->hgqk', query, keys))
    scores = jnp.where(allowed, scores, -1e+30)
    row_max = lax.optimization_barrier(jnp.max(scores, axis=-1, keepdims=True))
    lifted = jnp.exp(scores - row_max)
    probs = low(lifted / lax.optimization_barrier(jnp.sum(lifted, axis=-1, keepdims=True)))
    return contract('hgqk,khd->qhgd', probs, values)

def feed_forward(hidden, gain, gate_up_w, down_w):
    normed = low(norm_rows(hidden, gain))
    gate_up = low_back(contract('sd,dkf->skf', normed, gate_up_w))
    product = low(glu(gate_up))
    return hidden + low_back(matmul(product, down_w))

def forward(weights, hidden, segment_ids):
    gain_rows, kernel, w_in, w_out, gu_a, dn_a, w_query, w_kv, w_attn, gu_b, dn_b = weights
    length = hidden.shape[0]
    positions = doc_positions(segment_ids)
    normed = low(norm_rows(hidden, gain_rows[0]))
    mixed = low_back(contract('sd,dkc->skc', normed, w_in))
    conv_out = low(conv_mix(mixed, kernel, segment_ids))
    hidden = hidden + low_back(matmul(conv_out, w_out))
    hidden = feed_forward(hidden, gain_rows[1], gu_a, dn_a)
    normed = low(norm_rows(hidden, gain_rows[2]))
    query = low_back(matmul(normed, w_query))
    key_value = low_back(contract('sd,dkc->skc', normed, w_kv))
    query_rot = low(rope(query.reshape(length, H, HD), positions)).reshape(length, KV, H // KV, HD)
    keys_rot = low(rope(key_value[:, 0].reshape(length, KV, HD), positions))
    values = low(key_value[:, 1].reshape(length, KV, HD))
    attended = jax.checkpoint(attention_core)(query_rot, keys_rot, values, segment_ids)
    attended = low(low_back(attended.reshape(length, H * HD)))
    hidden = hidden + low_back(matmul(attended, w_attn))
    return feed_forward(hidden, gain_rows[3], gu_b, dn_b)

def reference(tokens_in, segments, gains, taps, in_proj, out_proj, gate_up_a, down_a, query_w, key_value_w, attn_out_w, gate_up_b, down_b, cotangent):
    params = tuple((weight.astype(jnp.float32) for weight in (gains, taps, in_proj, out_proj, gate_up_a, down_a, query_w, key_value_w, attn_out_w, gate_up_b, down_b)))

    def one_sequence(totals, inputs):
        seq_tokens, seq_segments, seq_cotangent = inputs
        seq_output, pullback = jax.vjp(lambda weights, hidden: forward(weights, hidden, seq_segments), params, seq_tokens)
        grad_weights, grad_hidden = pullback(seq_cotangent)
        totals = jax.tree.map(jnp.add, totals, grad_weights)
        return (totals, (seq_output.astype(jnp.bfloat16), grad_hidden))
    start_totals = jax.tree.map(jnp.zeros_like, params)
    totals, (output, grad_input) = lax.scan(one_sequence, start_totals, (tokens_in.astype(jnp.float32), segments, cotangent.astype(jnp.float32)))
    return (output, grad_input, totals[0], totals[1], totals[2], totals[3], totals[4], totals[5], totals[6], totals[7], totals[8], totals[9], totals[10])
```

```python
import math

import jax
import jax.numpy as jnp
from jax import lax
from jax.sharding import PartitionSpec as P

HD = 64
EPS = 1e-05
THETA = 1000000.0
SCALE = 0.125
BF = jnp.bfloat16
F32 = jnp.float32


def flip(values, bit):
    n = lax.axis_size("dp")
    return lax.ppermute(values, "dp", [(i, i ^ bit) for i in range(n)])


def turn(values, step):
    n = lax.axis_size("dp")
    return lax.ppermute(values, "dp", [(i, (i + 4 * step) % n) for i in range(n)])


def swap(values):
    return lax.ppermute(values, "tensor", [(0, 1), (1, 0)])


def z_gather(own):
    nz = lax.axis_size("dp") // 4
    blocks = [own] + [None] * (nz - 1)
    from_above = from_below = own
    for r in range(1, nz // 2 + 1):
        from_above = turn(from_above, -1)
        blocks[r] = from_above
        if nz - r > r:
            from_below = turn(from_below, 1)
            blocks[nz - r] = from_below
    return blocks


def z_scatter(blocks):
    nz = len(blocks)
    half = nz // 2
    up = blocks[half]
    for r in range(half - 1, 0, -1):
        up = add_low(blocks[r], turn(up, 1))
    down = blocks[half + 1]
    for r in range(half + 2, nz):
        down = add_low(blocks[r], turn(down, -1))
    return blocks[0].astype(F32) + turn(up, 1).astype(F32) + turn(down, -1).astype(F32)


def add_low(a, b):
    return (a.astype(F32) + b.astype(F32)).astype(BF)


def gather_z_first(own, far):
    base = jnp.concatenate(z_gather(own), axis=0)
    by_x = flip(base, 1)
    by_y = flip(base, 2)
    by_xy = flip(by_x, 2) if far == "y" else flip(by_y, 1)
    return jnp.concatenate([base, by_x, by_y, by_xy], axis=0)


def gather_z_last(own, far):
    by_x = flip(own, 1)
    by_y = flip(own, 2)
    by_xy = flip(by_x, 2) if far == "y" else flip(by_y, 1)
    blocks = z_gather(jnp.stack([own, by_x, by_y, by_xy]))
    full = jnp.stack(blocks, axis=1)
    return full.reshape(-1, own.shape[-1])


def flip_scatter(parts, far):
    if far == "y":
        one = add_low(parts[1], flip(parts[3], 2))
        return parts[0].astype(F32) + flip(one, 1).astype(F32) + flip(parts[2], 2).astype(F32)
    two = add_low(parts[2], flip(parts[3], 1))
    return parts[0].astype(F32) + flip(two, 2).astype(F32) + flip(parts[1], 1).astype(F32)


def scatter_z_last(grad, far):
    nz = lax.axis_size("dp") // 4
    quarter = grad.shape[0] // 4
    rows = quarter // nz
    mine = flip_scatter([grad[j * quarter : (j + 1) * quarter] for j in range(4)], far).astype(BF)
    return z_scatter([mine[r * rows : (r + 1) * rows] for r in range(nz)])


def scatter_z_first(grad, far):
    nz = lax.axis_size("dp") // 4
    rows = grad.shape[0] // (4 * nz)
    blocks = grad.reshape(4, nz, rows, grad.shape[1])
    mine = z_scatter([blocks[:, r] for r in range(nz)]).astype(BF)
    return flip_scatter([mine[j] for j in range(4)], far)


def dot_nn(a, w):
    return jnp.dot(a, w, preferred_element_type=F32)


def dot_nt(a, w):
    return lax.dot_general(a, w, (((1,), (1,)), ((), ())), preferred_element_type=F32)


def dot_tn(a, b):
    return lax.dot_general(a, b, (((0,), (0,)), ((), ())), preferred_element_type=F32)


def inv_rms(values):
    return lax.rsqrt(jnp.mean(values * values, axis=-1, keepdims=True) + EPS)


def norm_low(values, gain):
    return (values * inv_rms(values) * gain).astype(BF)


def norm_back(grad_normed, values, gain, grad_out):
    q = inv_rms(values)
    grad_gain = jnp.sum(grad_normed * values * q, axis=0)
    a2 = grad_normed * gain
    inner = jnp.mean(a2 * values, axis=-1, keepdims=True)
    return grad_out + q * a2 - values * (q * q * q * inner), grad_gain


def rope_tables(positions):
    half = HD // 2
    freq = jnp.exp(jnp.arange(half, dtype=F32) * (-2.0 * math.log(THETA) / (2 * half)))
    angle = positions[:, None] * freq[None, :]
    return jnp.cos(angle)[:, None, :], jnp.sin(angle)[:, None, :]


def rope(values, cosine, sine):
    half = HD // 2
    first, second = values[..., :half], values[..., half:]
    return jnp.concatenate([first * cosine - second * sine, second * cosine + first * sine], axis=-1)


def conv_mix(mixed, kernel, same_one, same_two):
    driven = mixed[0] * mixed[2]
    zero = jnp.zeros((2, driven.shape[1]), driven.dtype)
    back_one = jnp.concatenate([zero[:1], driven[:-1]], axis=0) * same_one
    back_two = jnp.concatenate([zero, driven[:-2]], axis=0) * same_two
    return mixed[1] * (kernel[0] * driven + kernel[1] * back_one + kernel[2] * back_two)


def allowed_mask(segment_ids, start, block):
    length = segment_ids.shape[0]
    row_index = start + jnp.arange(block)
    col_index = jnp.arange(length)
    row_segs = segment_ids[start : start + block]
    return (col_index[None, :] <= row_index[:, None]) & (segment_ids[None, :] == row_segs[:, None])


def attend_forward(q_block, keys, values, allowed):
    scores = SCALE * jnp.einsum("qhgd,khd->hgqk", q_block, keys, preferred_element_type=F32)
    scores = jnp.where(allowed, scores, -1e30)
    row_max = jnp.max(scores, axis=-1, keepdims=True)
    lifted = jnp.exp(scores - row_max)
    row_total = jnp.sum(lifted, axis=-1, keepdims=True)
    probs = (lifted / row_total).astype(BF)
    attended = jnp.einsum("hgqk,khd->qhgd", probs, values, preferred_element_type=F32)
    return (attended, row_max + jnp.log(row_total))


def attend_backward(q_block, keys, values, allowed, log_total, grad_block):
    scores = SCALE * jnp.einsum("qhgd,khd->hgqk", q_block, keys, preferred_element_type=F32)
    probs = jnp.exp(jnp.where(allowed, scores, -1e30) - log_total)
    grad_values = jnp.einsum("hgqk,qhgd->khd", probs.astype(BF), grad_block, preferred_element_type=F32)
    grad_probs = jnp.einsum("qhgd,khd->hgqk", grad_block, values, preferred_element_type=F32)
    grad_scores = (
        probs * (grad_probs - jnp.sum(probs * grad_probs, axis=-1, keepdims=True))
    ).astype(BF)
    grad_query = SCALE * jnp.einsum("hgqk,khd->qhgd", grad_scores, keys, preferred_element_type=F32)
    grad_keys = SCALE * jnp.einsum("hgqk,qhgd->khd", grad_scores, q_block, preferred_element_type=F32)
    return (grad_query, grad_keys, grad_values)


def per_device(
    tokens_in,
    segments,
    gains,
    taps,
    in_proj,
    out_proj,
    gate_up_a,
    down_a,
    query_w,
    key_value_w,
    attn_out_w,
    gate_up_b,
    down_b,
    cotangent,
):
    half = tokens_in.shape[1]
    segment_ids = segments[0]
    length = segment_ids.shape[0]
    dp_size = lax.axis_size("dp")
    nz = dp_size // 4
    rows = in_proj.shape[0]
    width = rows * dp_size
    rank = lax.axis_index("tensor")
    me = lax.axis_index("dp")

    flips = jnp.arange(dp_size) // nz
    steps = jnp.arange(dp_size) % nz
    owner = ((me // 4 + steps) % nz) * 4 + ((me % 4) ^ flips)
    place = (owner[:, None] * rows + jnp.arange(rows)[None, :]).reshape(width)
    to_rel = (jnp.arange(width)[:, None] == place[None, :]).astype(BF)

    def both(own):
        return jnp.concatenate([own, swap(own)], axis=0)

    def in_order(own):
        other = swap(own)
        first = jnp.where(rank == 0, own, other)
        second = jnp.where(rank == 0, other, own)
        return jnp.concatenate([first, second], axis=0)

    def own_half(full):
        return lax.dynamic_slice_in_dim(full, rank * half, half, 0)

    def other_half(full):
        return lax.dynamic_slice_in_dim(full, (1 - rank) * half, half, 0)

    misc = jnp.concatenate(
        [gains.T, taps.T, jnp.zeros((rows, 128 - gains.shape[0] - taps.shape[0]), BF)], axis=1
    )
    conv_cols = in_proj.shape[2]
    first_item = gather_z_first(
        jnp.concatenate([misc] + [in_proj[:, k] for k in range(3)], axis=1), "y"
    )
    w_out = gather_z_last(out_proj.T, "x")
    misc_all = first_item[:, :128]
    w_in = [first_item[:, 128 + k * conv_cols : 128 + (k + 1) * conv_cols] for k in range(3)]

    def gather_ff(gate_up, down):
        gate = gather_z_first(gate_up[:, 0], "y")
        up = gather_z_first(gate_up[:, 1], "x")
        down_t = down.T
        cut = down_t.shape[1] // 2
        one = gather_z_last(down_t[:, :cut], "y")
        two = gather_z_first(down_t[:, cut:], "x")
        return gate, up, jnp.concatenate([one, two], axis=1)

    ff_a = gather_ff(gate_up_a, down_a)
    query_cols = query_w.shape[1]
    kv_cols = key_value_w.shape[2]
    w_qkv = gather_z_first(
        jnp.concatenate([query_w, key_value_w[:, 0], key_value_w[:, 1]], axis=1), "y"
    )
    w_attn = gather_z_last(attn_out_w.T, "x")
    ff_b = gather_ff(gate_up_b, down_b)

    gain_rows = misc_all[:, : gains.shape[0]].T.astype(F32)
    taps_all = lax.dot_general(
        misc_all[:, 4:7], to_rel, (((0,), (1,)), ((), ())), preferred_element_type=F32
    )
    kernel = lax.dynamic_slice_in_dim(taps_all, rank * conv_cols, conv_cols, 1)

    index = jnp.arange(length)
    first_of_doc = jnp.sum((segment_ids[None, :] < segment_ids[:, None]).astype(jnp.int32), axis=1)
    positions = (index - first_of_doc).astype(F32)
    same_one = (positions >= 1).astype(F32)[:, None]
    same_two = (positions >= 2).astype(F32)[:, None]
    cosine, sine = rope_tables(positions)

    hidden_zero = dot_nn(tokens_in[0], to_rel)
    first_full = in_order(norm_low(hidden_zero, gain_rows[0]))
    mixed = [dot_nn(first_full, w) for w in w_in]
    conv_out, conv_pull = jax.vjp(
        lambda mixed_in, kernel_in: conv_mix(mixed_in, kernel_in, same_one, same_two), mixed, kernel
    )
    conv_low = conv_out.astype(BF)

    def collect(own, other, w):
        sent = swap(dot_nt(other, w).astype(BF))
        return dot_nt(own, w) + sent.astype(F32)

    hidden_one = hidden_zero + collect(own_half(conv_low), other_half(conv_low), w_out)

    def feed_forward(hidden, gain, weights):
        w_gate, w_up, w_down = weights
        normed = both(norm_low(hidden, gain))
        gate = dot_nn(normed, w_gate)
        up = dot_nn(normed, w_up)
        product = (jax.nn.silu(gate) * up).astype(BF)
        gate, up = gate.astype(BF), up.astype(BF)
        return hidden + collect(product[:half], product[half:], w_down), (normed, gate, up, product)

    def feed_back(grad_out, hidden, gain, weights, kept):
        w_gate, w_up, w_down = weights
        normed, gate, up, product = kept
        grad_full = both(grad_out.astype(BF))
        grad_product = dot_nn(grad_full, w_down)
        gate, up = gate.astype(F32), up.astype(F32)
        sig = jax.nn.sigmoid(gate)
        grad_up = (grad_product * (gate * sig)).astype(BF)
        grad_gate = (grad_product * up * (sig * (1.0 + gate * (1.0 - sig)))).astype(BF)
        g_down = dot_tn(grad_full, product).astype(BF)
        g_gate = dot_tn(normed, grad_gate).astype(BF)
        g_up = dot_tn(normed, grad_up).astype(BF)
        sent = swap((dot_nt(grad_gate[half:], w_gate) + dot_nt(grad_up[half:], w_up)).astype(BF))
        grad_normed = (
            dot_nt(grad_gate[:half], w_gate) + dot_nt(grad_up[:half], w_up) + sent.astype(F32)
        )
        grad_hidden, grad_gain = norm_back(grad_normed, hidden, gain, grad_out)
        return grad_hidden, grad_gain, (g_gate, g_up, g_down)

    def scatter_ff(grads):
        g_gate, g_up, g_down = grads
        cut = g_down.shape[1] // 2
        one = scatter_z_first(g_down[:, :cut], "y")
        two = scatter_z_last(g_down[:, cut:], "x")
        gate = scatter_z_last(g_gate, "y")
        up = scatter_z_last(g_up, "x")
        return jnp.stack([gate, up], axis=1), jnp.concatenate([one, two], axis=1).T

    hidden_two, kept_a = feed_forward(hidden_one, gain_rows[1], ff_a)

    heads_local = query_cols // HD
    kv_local = kv_cols // HD
    group = heads_local // kv_local
    third_full = in_order(norm_low(hidden_two, gain_rows[2]))
    qkv = dot_nn(third_full, w_qkv)
    query_low = rope(qkv[:, :query_cols].reshape(length, heads_local, HD), cosine, sine)
    query_low = query_low.astype(BF).reshape(length, kv_local, group, HD)
    keys_low = rope(
        qkv[:, query_cols : query_cols + kv_cols].reshape(length, kv_local, HD), cosine, sine
    ).astype(BF)
    values_low = qkv[:, query_cols + kv_cols :].reshape(length, kv_local, HD).astype(BF)
    block = min(512, length)
    attended_parts = []
    log_totals = []
    for start in range(0, length, block):
        stop = start + block
        allowed = allowed_mask(segment_ids, start, block)[:, :stop]
        attended, log_total = attend_forward(
            query_low[start:stop], keys_low[:stop], values_low[:stop], allowed
        )
        attended_parts.append(attended)
        log_totals.append(log_total)
    attended_low = jnp.concatenate(attended_parts, axis=0).reshape(length, query_cols).astype(BF)
    hidden_three = hidden_two + collect(own_half(attended_low), other_half(attended_low), w_attn)
    hidden_four, kept_b = feed_forward(hidden_three, gain_rows[3], ff_b)
    output = dot_nt(hidden_four.astype(BF), to_rel).astype(BF)[None]

    grad_four = dot_nn(cotangent[0], to_rel)
    grad_three, gain_grad_three, grads_b = feed_back(
        grad_four, hidden_three, gain_rows[3], ff_b, kept_b
    )
    summed_gu_b, summed_dn_b = scatter_ff(grads_b)
    attn_full = in_order(grad_three.astype(BF))
    grad_attn = dot_tn(attn_full, attended_low).astype(BF)
    grad_attended = dot_nn(attn_full, w_attn).astype(BF).reshape(length, kv_local, group, HD)
    grad_keys = jnp.zeros((length, kv_local, HD), F32)
    grad_values = jnp.zeros((length, kv_local, HD), F32)
    query_grads = []
    for block_index, start in enumerate(range(0, length, block)):
        stop = start + block
        allowed = allowed_mask(segment_ids, start, block)[:, :stop]
        grad_query, keys_part, values_part = attend_backward(
            query_low[start:stop],
            keys_low[:stop],
            values_low[:stop],
            allowed,
            log_totals[block_index],
            grad_attended[start:stop],
        )
        query_grads.append(grad_query)
        pad = ((0, length - stop), (0, 0), (0, 0))
        grad_keys = grad_keys + jnp.pad(keys_part, pad)
        grad_values = grad_values + jnp.pad(values_part, pad)
    grad_query_rot = jnp.concatenate(query_grads, axis=0).reshape(length, heads_local, HD)
    grad_qkv = jnp.concatenate(
        [
            rope(grad_query_rot, cosine, -sine).reshape(length, query_cols).astype(BF),
            rope(grad_keys, cosine, -sine).reshape(length, kv_cols).astype(BF),
            grad_values.reshape(length, kv_cols).astype(BF),
        ],
        axis=1,
    )
    grad_wqkv = dot_tn(third_full, grad_qkv).astype(BF)
    grad_third = collect(own_half(grad_qkv), other_half(grad_qkv), w_qkv)
    grad_two, gain_grad_two = norm_back(grad_third, hidden_two, gain_rows[2], grad_three)
    summed_qkv = scatter_z_last(grad_wqkv, "y")
    summed_attn = scatter_z_first(grad_attn, "x").T

    grad_one, gain_grad_one, grads_a = feed_back(
        grad_two, hidden_one, gain_rows[1], ff_a, kept_a
    )
    summed_gu_a, summed_dn_a = scatter_ff(grads_a)
    conv_full = in_order(grad_one.astype(BF))
    grad_wout = dot_tn(conv_full, conv_low).astype(BF)
    grad_conv = dot_nn(conv_full, w_out)
    grad_mixed, grad_kernel = conv_pull(grad_conv)
    grad_mixed = [g.astype(BF) for g in grad_mixed]
    own_first = sum(dot_nt(own_half(g), w) for g, w in zip(grad_mixed, w_in))
    other_first = sum(dot_nt(other_half(g), w) for g, w in zip(grad_mixed, w_in))
    grad_first = own_first + swap(other_first.astype(BF)).astype(F32)
    grad_zero, gain_grad_zero = norm_back(grad_first, hidden_zero, gain_rows[0], grad_one)

    high = grad_zero.astype(BF)
    lower = (grad_zero - high.astype(F32)).astype(BF)
    grad_input = (dot_nt(high, to_rel) + dot_nt(lower, to_rel))[None]

    kernel_full = lax.dynamic_update_slice(
        jnp.zeros((3, width), F32), grad_kernel, (0, rank * conv_cols)
    )
    kernel_rel = dot_nn(kernel_full.astype(BF), to_rel)
    small = jnp.concatenate(
        [
            jnp.stack([gain_grad_zero, gain_grad_one, gain_grad_two, gain_grad_three]),
            kernel_rel,
            jnp.zeros((128 - 7, width), F32),
        ],
        axis=0,
    ).T.astype(BF)
    grad_win = [dot_tn(first_full, g).astype(BF) for g in grad_mixed]
    summed_first = scatter_z_last(jnp.concatenate([small] + grad_win, axis=1), "y")
    summed_wout = scatter_z_first(grad_wout, "x").T
    summed_win = summed_first[:, 128:].reshape(rows, 3, conv_cols)
    small_sum = summed_first[:, :128]
    small_sum = (small_sum + swap(small_sum)).T
    return (
        output,
        grad_input,
        small_sum[:4],
        small_sum[4:7],
        summed_win,
        summed_wout,
        summed_gu_a,
        summed_dn_a,
        summed_qkv[:, :query_cols],
        summed_qkv[:, query_cols:].reshape(rows, 2, kv_cols),
        summed_attn,
        summed_gu_b,
        summed_dn_b,
    )


def solution(mesh):
    return jax.shard_map(
        per_device,
        mesh=mesh,
        in_specs=(
            P("dp", "tensor", None),
            P("dp", None),
            P(None, "dp"),
            P(None, "dp"),
            P("dp", None, "tensor"),
            P("tensor", "dp"),
            P("dp", None, "tensor"),
            P("tensor", "dp"),
            P("dp", "tensor"),
            P("dp", None, "tensor"),
            P("tensor", "dp"),
            P("dp", None, "tensor"),
            P("tensor", "dp"),
            P("dp", "tensor", None),
        ),
        out_specs=(
            P("dp", "tensor", None),
            P("dp", "tensor", None),
            P(None, "dp"),
            P(None, "dp"),
            P("dp", None, "tensor"),
            P("tensor", "dp"),
            P("dp", None, "tensor"),
            P("tensor", "dp"),
            P("dp", "tensor"),
            P("dp", None, "tensor"),
            P("tensor", "dp"),
            P("dp", None, "tensor"),
            P("tensor", "dp"),
        ),
        check_vma=False,
    )
```

```python
import functools
import math

import jax
import jax.numpy as jnp
from jax import lax
from jax.experimental import pallas as pl
from jax.experimental.pallas import tpu as pltpu
from jax.sharding import PartitionSpec as P

HD = 64
EPS = 1e-05
THETA = 1000000.0
SCALE = 0.125
BF = jnp.bfloat16
F32 = jnp.float32


def ring():
    count = lax.axis_size("dp") // 2
    return [0] + list(range(1, count, 2)) + list(range(count - 2, 0, -2))


def ring_groups():
    return [[2 * k + x for k in ring()] for x in range(2)]


def swap(values):
    return lax.ppermute(values, "tensor", [(0, 1), (1, 0)])


def flip_x(values):
    n = lax.axis_size("dp")
    return lax.ppermute(values, "dp", [(i, i ^ 1) for i in range(n)])


def by_x(mine, theirs, axis):
    x_bit = lax.axis_index("dp") % 2
    return jnp.concatenate(
        [jnp.where(x_bit == 0, mine, theirs), jnp.where(x_bit == 0, theirs, mine)], axis=axis
    )


def halves(values, axis):
    x_bit = lax.axis_index("dp") % 2
    left, right = jnp.split(values, 2, axis=axis)
    return jnp.where(x_bit == 0, left, right), jnp.where(x_bit == 0, right, left)


def ring_gather(pair):
    return lax.all_gather(pair, "dp", axis=0, axis_index_groups=ring_groups(), tiled=True)


def ring_sum(grad):
    return lax.psum_scatter(
        grad, "dp", scatter_dimension=0, axis_index_groups=ring_groups(), tiled=True
    )


def ring_order(values, axis, back=False):
    order = ring()
    if back:
        order = [order.index(k) for k in range(len(order))]
    size = values.shape[axis] // len(order)
    return jnp.concatenate(
        [lax.slice_in_dim(values, k * size, (k + 1) * size, axis=axis) for k in order], axis=axis
    )


def dot_nn(a, w):
    return jnp.dot(a, w, preferred_element_type=F32)


def dot_nt(a, w):
    return lax.dot_general(a, w, (((1,), (1,)), ((), ())), preferred_element_type=F32)


def dot_tn(a, b):
    return lax.dot_general(a, b, (((0,), (0,)), ((), ())), preferred_element_type=F32)


def params(steps=1):
    return pltpu.CompilerParams(
        vmem_limit_bytes=48 * 2**20, dimension_semantics=("arbitrary",) * steps
    )


def whole(array):
    return pl.BlockSpec(array.shape, lambda *_: (0, 0), pipeline_mode=pl.Buffered(1))


def column(array, cols, at):
    return pl.BlockSpec((array.shape[0], cols), lambda *_: (0, at), pipeline_mode=pl.Buffered(1))


def cost(flops, *arrays):
    return pl.CostEstimate(
        flops=flops,
        bytes_accessed=sum(a.size * a.dtype.itemsize for a in arrays),
        transcendentals=0,
    )


def ff_up_kernel(h0, h1, wg, wu, gate_ref, up_ref, product_ref):
    i = pl.program_id(0)

    def step(h):
        gate = jnp.dot(h[...], wg[...], preferred_element_type=F32)
        up = jnp.dot(h[...], wu[...], preferred_element_type=F32)
        gate_ref[...] = gate.astype(BF)
        up_ref[...] = up.astype(BF)
        product_ref[...] = (gate / (1.0 + jnp.exp(-gate)) * up).astype(BF)

    pl.when(i == 0)(lambda: step(h0))
    pl.when(i == 1)(lambda: step(h1))


def ff_up(h0, h1, weights, cols):
    rows, depth = h0.shape
    out = jax.ShapeDtypeStruct((2 * rows, cols), BF)
    tile = pl.BlockSpec((rows, cols), lambda i: (i, 0))
    return pl.pallas_call(
        ff_up_kernel,
        grid=(2,),
        out_shape=(out, out, out),
        in_specs=[whole(h0), whole(h1), column(weights, cols, 0), column(weights, cols, 1)],
        out_specs=(tile, tile, tile),
        compiler_params=params(),
        cost_estimate=cost(8 * rows * depth * cols, h0, h1, out, out, out, out, out),
    )(h0, h1, weights, weights)


def ff_back_kernel(e0, e1, wd, gate_ref, up_ref, dgate_ref, dup_ref):
    i = pl.program_id(0)

    def step(e):
        da = jnp.dot(e[...], wd[...], preferred_element_type=F32)
        gate = gate_ref[...].astype(F32)
        up = up_ref[...].astype(F32)
        sig = 1.0 / (1.0 + jnp.exp(-gate))
        lit = gate * sig
        dup_ref[...] = (da * lit).astype(BF)
        dgate_ref[...] = (da * up * (sig + lit - lit * sig)).astype(BF)

    pl.when(i == 0)(lambda: step(e0))
    pl.when(i == 1)(lambda: step(e1))


def ff_back(e0, e1, weights, gate, up):
    rows, depth = e0.shape
    cols = gate.shape[1]
    out = jax.ShapeDtypeStruct((2 * rows, cols), BF)
    tile = pl.BlockSpec((rows, cols), lambda i: (i, 0))
    return pl.pallas_call(
        ff_back_kernel,
        grid=(2,),
        out_shape=(out, out),
        in_specs=[whole(e0), whole(e1), column(weights, cols, 2), tile, tile],
        out_specs=(tile, tile),
        compiler_params=params(),
        cost_estimate=cost(4 * rows * depth * cols, e0, e1, gate, gate, up, out, out),
    )(e0, e1, weights, gate, up)


def weight_grad_kernel(*refs):
    left, right, out_ref = refs[:4], refs[4:-1], refs[-1]
    rows = left[0].shape[0]
    cols = right[0].shape[1]
    turned = [l[...].T for l in left]
    for k in range(len(right) // 2):
        near, far = right[2 * k], right[2 * k + 1]
        total = jnp.dot(turned[0], near[:rows], preferred_element_type=F32)
        total += jnp.dot(turned[1], near[rows:], preferred_element_type=F32)
        total += jnp.dot(turned[2], far[:rows], preferred_element_type=F32)
        total += jnp.dot(turned[3], far[rows:], preferred_element_type=F32)
        out_ref[:, k * cols : (k + 1) * cols] = total.astype(BF)


def weight_grad(left, right):
    rows, depth = left[0].shape
    tile = 256
    cols = right[0][0].shape[1] * len(right)
    flat = [r for pair in right for r in pair]
    out = jax.ShapeDtypeStruct((depth, cols), BF)
    return pl.pallas_call(
        weight_grad_kernel,
        grid=(depth // tile,),
        out_shape=out,
        in_specs=[pl.BlockSpec((rows, tile), lambda i: (0, i))] * 4 + [whole(r) for r in flat],
        out_specs=pl.BlockSpec((tile, cols), lambda i: (i, 0)),
        compiler_params=params(),
        cost_estimate=cost(8 * rows * depth * cols, *left, *flat, out),
    )(*left, *flat)


def narrow_kernel(n, *refs):
    left, right, keep_ref, send_ref = refs[:n], refs[n : 2 * n], refs[2 * n], refs[2 * n + 1]
    rows = keep_ref.shape[0]

    def total(part):
        t = None
        for l, r in zip(left, right):
            v = lax.dot_general(l[part], r[...], (((1,), (1,)), ((), ())), preferred_element_type=F32)
            t = v if t is None else t + v
        return t

    send_ref[...] = total(pl.ds(rows, rows)).astype(BF)
    keep_ref[...] = total(pl.ds(0, rows))


def narrow(left, weights, places):
    rows, cols = left[0].shape
    depth = weights.shape[0]
    n = len(left)
    tile = 256
    keep = jax.ShapeDtypeStruct((rows // 2, depth), F32)
    send = jax.ShapeDtypeStruct((rows // 2, depth), BF)
    out = pl.BlockSpec((rows // 2, tile), lambda i: (0, i))
    parts = [pl.BlockSpec((tile, cols), functools.partial(lambda at, i: (i, at), p)) for p in places]
    return pl.pallas_call(
        functools.partial(narrow_kernel, n),
        grid=(depth // tile,),
        out_shape=(keep, send),
        in_specs=[whole(l) for l in left] + parts,
        out_specs=(out, out),
        compiler_params=params(),
        cost_estimate=cost(2 * rows * depth * cols * n, *left, *left, keep, send),
    )(*left, *[weights] * n)


def turn_heads(values, cosine, sine):
    half = HD // 2
    first, second = values[:half], values[half:]
    return jnp.concatenate([first * cosine - second * sine, second * cosine + first * sine], axis=0)


def allowed_keys(start_ref, begin, stop):
    shape = (stop, stop - begin)
    key = lax.broadcasted_iota(jnp.int32, shape, 0)
    query = begin + lax.broadcasted_iota(jnp.int32, shape, 1)
    return (key <= query) & (key >= start_ref[:, begin:stop])


def attend_kernel(block, start_ref, cos_ref, sin_ref, q_ref, k_ref, v_ref, qr_ref, kr_ref, vr_ref, o_ref, log_ref):
    length = q_ref.shape[1]
    cosine, sine = cos_ref[...], sin_ref[...]
    keys = turn_heads(k_ref[...], cosine, sine).astype(BF)
    values = v_ref[...].astype(BF)
    kr_ref[...] = keys
    vr_ref[...] = values
    keys_down = keys.T
    for g in range(q_ref.shape[0] // HD):
        head = slice(g * HD, (g + 1) * HD)
        query = turn_heads(q_ref[head, :], cosine, sine).astype(BF) * jnp.asarray(SCALE, BF)
        qr_ref[head, :] = query
        for begin in range(0, length, block):
            stop = begin + block
            scores = jnp.dot(keys_down[:stop], query[:, begin:stop], preferred_element_type=F32)
            scores = jnp.where(allowed_keys(start_ref, begin, stop), scores, -1e30)
            top = jnp.max(scores, axis=0, keepdims=True)
            lifted = jnp.exp(scores - top)
            total = jnp.sum(lifted, axis=0, keepdims=True)
            probs = (lifted * (1.0 / total)).astype(BF)
            out = jnp.dot(values[:, :stop], probs, preferred_element_type=F32)
            o_ref[head, begin:stop] = out.astype(BF)
            log_ref[0, g : g + 1, begin:stop] = top + jnp.log(total)


def attend(start, cosine, sine, qkv, query_rows, kv_rows):
    length = qkv.shape[1]
    heads = kv_rows // HD
    group = query_rows // heads
    q_spec = pl.BlockSpec((group, length), lambda h: (h, 0))
    out_spec = pl.BlockSpec((HD, length), lambda h: (h, 0))
    k_at, v_at = query_rows // HD, (query_rows + kv_rows) // HD
    q_out = jax.ShapeDtypeStruct((query_rows, length), BF)
    kv_out = jax.ShapeDtypeStruct((kv_rows, length), BF)
    return pl.pallas_call(
        functools.partial(attend_kernel, min(256, length)),
        grid=(heads,),
        out_shape=(q_out, kv_out, kv_out, q_out, jax.ShapeDtypeStruct((heads, group // HD, length), F32)),
        in_specs=[
            whole(start),
            whole(cosine),
            whole(sine),
            q_spec,
            pl.BlockSpec((HD, length), lambda h: (k_at + h, 0)),
            pl.BlockSpec((HD, length), lambda h: (v_at + h, 0)),
        ],
        out_specs=(
            q_spec,
            out_spec,
            out_spec,
            q_spec,
            pl.BlockSpec((1, group // HD, length), lambda h: (h, 0, 0)),
        ),
        compiler_params=params(),
        cost_estimate=cost(2 * query_rows * length * length, qkv, qkv),
    )(start, cosine, sine, qkv, qkv, qkv)


def attend_back_kernel(
    block, start_ref, cos_ref, sin_ref, q_ref, k_ref, v_ref, log_ref, do_ref, dq_ref, dk_ref, dv_ref, dk_sum, dv_sum
):
    length = q_ref.shape[1]
    cosine, sine = cos_ref[...], sin_ref[...]
    keys = k_ref[...]
    keys_down = keys.T
    values_down = v_ref[...].T
    dk_sum[...] = jnp.zeros_like(dk_sum)
    dv_sum[...] = jnp.zeros_like(dv_sum)
    over_rows = (((1,), (1,)), ((), ()))
    for g in range(q_ref.shape[0] // HD):
        head = slice(g * HD, (g + 1) * HD)
        parts = []
        for begin in range(0, length, block):
            stop = begin + block
            query = q_ref[head, begin:stop]
            grad = do_ref[head, begin:stop]
            scores = jnp.dot(keys_down[:stop], query, preferred_element_type=F32)
            scores = jnp.where(allowed_keys(start_ref, begin, stop), scores, -1e30)
            probs = jnp.exp(scores - log_ref[0, g : g + 1, begin:stop])
            grad_probs = jnp.dot(values_down[:stop], grad, preferred_element_type=F32)
            inner = jnp.sum(probs * grad_probs, axis=0, keepdims=True)
            grad_scores = (probs * (grad_probs - inner)).astype(BF)
            parts.append(jnp.dot(keys[:, :stop], grad_scores, preferred_element_type=F32))
            dk_sum[:, :stop] += lax.dot_general(query, grad_scores, over_rows, preferred_element_type=F32)
            dv_sum[:, :stop] += lax.dot_general(grad, probs.astype(BF), over_rows, preferred_element_type=F32)
        whole_head = SCALE * jnp.concatenate(parts, axis=1)
        dq_ref[head, :] = turn_heads(whole_head, cosine, -sine).astype(BF)
    dk_ref[...] = turn_heads(dk_sum[...], cosine, -sine).astype(BF)
    dv_ref[...] = dv_sum[...].astype(BF)


def attend_back(start, cosine, sine, query, keys, values, logs, grad):
    query_rows, length = query.shape
    kv_rows = keys.shape[0]
    heads = kv_rows // HD
    group = query_rows // heads
    q_spec = pl.BlockSpec((group, length), lambda h: (h, 0))
    kv_spec = pl.BlockSpec((HD, length), lambda h: (h, 0))
    q_out = jax.ShapeDtypeStruct((query_rows, length), BF)
    kv_out = jax.ShapeDtypeStruct((kv_rows, length), BF)
    return pl.pallas_call(
        functools.partial(attend_back_kernel, min(256, length)),
        grid=(heads,),
        out_shape=(q_out, kv_out, kv_out),
        in_specs=[
            whole(start),
            whole(cosine),
            whole(sine),
            q_spec,
            kv_spec,
            kv_spec,
            pl.BlockSpec((1, group // HD, length), lambda h: (h, 0, 0)),
            q_spec,
        ],
        out_specs=(q_spec, kv_spec, kv_spec),
        scratch_shapes=[pltpu.VMEM((HD, length), F32), pltpu.VMEM((HD, length), F32)],
        compiler_params=params(),
        cost_estimate=cost(6 * query_rows * length * length, query, query, grad, grad),
    )(start, cosine, sine, query, keys, values, logs, grad)


def second_grads_kernel(count, *refs):
    left0, left1, rights, out_ref = refs[0], refs[1], refs[2:-1], refs[-1]
    over_rows = (((1,), (1,)), ((), ()))
    turned = left0[...].T, left1[...].T
    at = 0
    for k, right in enumerate(rights):
        got = lax.dot_general(turned[k >= count], right[...], over_rows, preferred_element_type=F32)
        out_ref[:, at : at + got.shape[1]] = got.astype(BF)
        at += got.shape[1]


def second_grads(left0, rights0, left1, right1):
    length, depth = left0.shape
    tile = 256
    rights = [*rights0, right1]
    cols = sum(r.shape[0] for r in rights)
    out = jax.ShapeDtypeStruct((depth, cols), BF)
    left = pl.BlockSpec((length, tile), lambda i: (0, i))
    return pl.pallas_call(
        functools.partial(second_grads_kernel, len(rights0)),
        grid=(depth // tile,),
        out_shape=out,
        in_specs=[left, left] + [whole(r) for r in rights],
        out_specs=pl.BlockSpec((tile, cols), lambda i: (i, 0)),
        compiler_params=params(),
        cost_estimate=cost(2 * length * depth * cols, left0, left1, *rights, out),
    )(left0, left1, *rights)


def first_grads_kernel(left0, left1, g0, g1, g2, low, small, out_ref):
    cols = g0.shape[1]
    turned = left0[...].T
    for k, right in enumerate((g0, g1, g2)):
        got = jnp.dot(turned, right[...], preferred_element_type=F32)
        out_ref[:, k * cols : (k + 1) * cols] = got.astype(BF)
    got = jnp.dot(left1[...].T, low[...], preferred_element_type=F32)
    out_ref[:, 3 * cols : 4 * cols] = got.astype(BF)
    out_ref[:, 4 * cols :] = small[...]


def first_grads(left0, rights, left1, low, small):
    length, depth = left0.shape
    tile = 256
    cols = low.shape[1]
    width = 4 * cols + small.shape[1]
    out = jax.ShapeDtypeStruct((depth, width), BF)
    left = pl.BlockSpec((length, tile), lambda i: (0, i))
    return pl.pallas_call(
        first_grads_kernel,
        grid=(depth // tile,),
        out_shape=out,
        in_specs=[left, left]
        + [whole(r) for r in (*rights, low)]
        + [pl.BlockSpec((tile, small.shape[1]), lambda i: (i, 0))],
        out_specs=pl.BlockSpec((tile, width), lambda i: (i, 0)),
        compiler_params=params(),
        cost_estimate=cost(8 * length * depth * cols, left0, left1, *rights, low, out),
    )(left0, left1, *rights, low, small)


def inv_rms(values):
    return lax.rsqrt(jnp.mean(values * values, axis=-1, keepdims=True) + EPS)


def norm_low(values, gain):
    return (values * inv_rms(values) * gain).astype(BF)


def norm_back(grad_normed, values, gain, grad_out):
    q = inv_rms(values)
    grad_gain = jnp.sum(grad_normed * values * q, axis=0)
    a2 = grad_normed * gain
    inner = jnp.mean(a2 * values, axis=-1, keepdims=True)
    return grad_out + q * a2 - values * (q * q * q * inner), grad_gain


def rope_tables(positions):
    half = HD // 2
    freq = jnp.exp(jnp.arange(half, dtype=F32) * (-2.0 * math.log(THETA) / (2 * half)))
    angle = freq[:, None] * positions[None, :]
    return jnp.cos(angle), jnp.sin(angle)


def conv_mix(mixed, kernel, same_one, same_two):
    driven = mixed[0] * mixed[2]
    zero = jnp.zeros((2, driven.shape[1]), driven.dtype)
    back_one = jnp.concatenate([zero[:1], driven[:-1]], axis=0) * same_one
    back_two = jnp.concatenate([zero, driven[:-2]], axis=0) * same_two
    return mixed[1] * (kernel[0] * driven + kernel[1] * back_one + kernel[2] * back_two)


def per_device(
    tokens_in,
    segments,
    gains,
    taps,
    in_proj,
    out_proj,
    gate_up_a,
    down_a,
    query_w,
    key_value_w,
    attn_out_w,
    gate_up_b,
    down_b,
    cotangent,
):
    half = tokens_in.shape[1]
    segment_ids = segments[0]
    length = segment_ids.shape[0]
    rows = in_proj.shape[0]
    width = rows * lax.axis_size("dp")
    rank = lax.axis_index("tensor")

    def in_order(own):
        other = swap(own)
        first = jnp.where(rank == 0, own, other)
        second = jnp.where(rank == 0, other, own)
        return jnp.concatenate([first, second], axis=0)

    def own_half(full):
        return lax.dynamic_slice_in_dim(full, rank * half, half, 0)

    def other_half(full):
        return lax.dynamic_slice_in_dim(full, (1 - rank) * half, half, 0)

    def four(own):
        far = flip_x(own)
        return own, swap(own), far, swap(far)

    def four_back(near, far):
        far_sum = (far[0] + swap(far[1]).astype(F32)).astype(BF)
        return near[0] + swap(near[1]).astype(F32) + flip_x(far_sum).astype(F32)

    misc = jnp.concatenate(
        [gains.T, taps.T, jnp.zeros((rows, 128 - gains.shape[0] - taps.shape[0]), BF)], axis=1
    )
    conv_cols = in_proj.shape[2]
    query_cols = query_w.shape[1]
    kv_cols = key_value_w.shape[2]
    unit = down_a.shape[0] // 2

    def shared(gate_up, down):
        parts = [halves(v, 1) for v in (gate_up[:, 0], gate_up[:, 1], down.T)]
        mine = jnp.concatenate([p[0] for p in parts], axis=1)
        return by_x(mine, flip_x(jnp.concatenate([p[1] for p in parts], axis=1)), 0)

    own = jnp.concatenate([in_proj[:, 0], in_proj[:, 1], in_proj[:, 2], out_proj.T, misc], axis=1)
    conv_w = ring_gather(by_x(own, flip_x(own), 0))
    ff_a = ring_gather(shared(gate_up_a, down_a))
    own = jnp.concatenate(
        [query_w, key_value_w[:, 0], key_value_w[:, 1], attn_out_w.T], axis=1
    )
    attn_w = ring_gather(by_x(own, flip_x(own), 0))
    ff_b = ring_gather(shared(gate_up_b, down_b))
    w_qkv = attn_w[:, : query_cols + 2 * kv_cols]
    w_attn = attn_w[:, query_cols + 2 * kv_cols :]
    w_in = [conv_w[:, k * conv_cols : (k + 1) * conv_cols] for k in range(3)]
    w_out = conv_w[:, 3 * conv_cols : 4 * conv_cols]
    misc_all = conv_w[:, 4 * conv_cols :]

    gain_rows = misc_all[:, :4].T.astype(F32)
    taps_all = ring_order(misc_all[:, 4:7].T, 1, back=True).astype(F32)
    kernel = lax.dynamic_slice_in_dim(taps_all, rank * conv_cols, conv_cols, 1)

    index = jnp.arange(length)
    first_of_doc = jnp.sum((segment_ids[None, :] < segment_ids[:, None]).astype(jnp.int32), axis=1)
    positions = (index - first_of_doc).astype(F32)
    same_one = (positions >= 1).astype(F32)[:, None]
    same_two = (positions >= 2).astype(F32)[:, None]
    cosine, sine = rope_tables(positions)
    doc_start = first_of_doc[None, :]

    hidden_zero = ring_order(tokens_in[0], 1).astype(F32)
    first_full = in_order(norm_low(hidden_zero, gain_rows[0]))
    grad_blocks = four(ring_order(cotangent[0], 1))
    first_full, grad_blocks = lax.optimization_barrier((first_full, grad_blocks))
    mixed = [dot_nn(first_full, w) for w in w_in]
    conv_out, conv_pull = jax.vjp(
        lambda mixed_in, kernel_in: conv_mix(mixed_in, kernel_in, same_one, same_two), mixed, kernel
    )
    conv_low = conv_out.astype(BF)

    def collect(own, other, w):
        sent = swap(dot_nt(other, w).astype(BF))
        return dot_nt(own, w) + sent.astype(F32)

    hidden_one = hidden_zero + collect(own_half(conv_low), other_half(conv_low), w_out)

    def feed_forward(hidden, gain, weights):
        blocks = four(norm_low(hidden, gain))
        near = ff_up(blocks[0], blocks[1], weights, unit)
        far = ff_up(blocks[2], blocks[3], weights, unit)
        return blocks, near, far

    def down(kept, weights):
        return narrow([kept[1][2]], weights, [2]), narrow([kept[2][2]], weights, [2])

    def feed_back(grad_out, grads, hidden, gain, weights, kept, settle):
        blocks, near, far = kept
        if len(grads) == 1:
            (own,) = grads
            sibling, across = swap(own), flip_x(own)
            near_back = ff_back(own, sibling, weights, near[0], near[1])
            near_sum = narrow(near_back, weights, [0, 1])
            near_sum, across = lax.optimization_barrier((near_sum, across))
            grads = own, sibling, across, swap(across)
        else:
            near_back = ff_back(grads[0], grads[1], weights, near[0], near[1])
            near_sum = narrow(near_back, weights, [0, 1])
        far_in = grads[2:]
        near_sum, far_in, settle = lax.optimization_barrier((near_sum, far_in, settle))
        far_back = ff_back(*far_in, weights, far[0], far[1])
        far_sum = narrow(far_back, weights, [0, 1])
        g_down = weight_grad(grads, [(near[2], far[2])])
        g_gate_up = weight_grad(
            blocks, [(near_back[0], far_back[0]), (near_back[1], far_back[1])]
        )
        grad_normed = four_back(near_sum, far_sum)
        grad_normed, g_down, g_gate_up = lax.optimization_barrier((grad_normed, g_down, g_gate_up))
        grad_hidden, grad_gain = norm_back(grad_normed, hidden, gain, grad_out)
        return grad_hidden, grad_gain, ring_sum(g_gate_up), ring_sum(g_down), settle

    def finish_shared(summed):
        mine, theirs = halves(summed, 0)
        return mine.astype(F32), flip_x(theirs).astype(F32)

    def finish(summed):
        mine, theirs = halves(summed, 0)
        return mine.astype(F32) + flip_x(theirs).astype(F32)

    def finish_ff(g_gate_up, g_down):
        down = finish_shared(g_down)
        mine, theirs = finish_shared(g_gate_up)
        gate = by_x(mine[:, :unit], theirs[:, :unit], 1)
        up = by_x(mine[:, unit:], theirs[:, unit:], 1)
        return jnp.stack([gate, up], axis=1), by_x(*down, 1).T

    kept_a = feed_forward(hidden_one, gain_rows[1], ff_a)
    hidden_two = hidden_one + four_back(*down(kept_a, ff_a))

    def my_part(full, other=False):
        start = (1 - rank if other else rank) * half
        return lax.dynamic_slice_in_dim(full, start, half, 1)

    def from_heads(full, w):
        over = (((0,), (1,)), ((), ()))
        sent = lax.dot_general(my_part(full, True), w, over, preferred_element_type=F32).astype(BF)
        kept = lax.dot_general(my_part(full), w, over, preferred_element_type=F32)
        return kept + swap(sent).astype(F32)

    def to_heads(w, full):
        return lax.dot_general(w, full, (((0,), (1,)), ((), ())), preferred_element_type=F32)

    third_full = in_order(norm_low(hidden_two, gain_rows[2]))
    qkv = to_heads(w_qkv, third_full)
    query, keys, values, attended, logs = attend(doc_start, cosine, sine, qkv, query_cols, kv_cols)
    hidden_three = hidden_two + from_heads(attended, w_attn)
    kept_b = feed_forward(hidden_three, gain_rows[3], ff_b)

    grad_four = ring_order(cotangent[0], 1).astype(F32)
    grad_three, gain_grad_three, sum_gu_b, sum_dn_b, _ = feed_back(
        grad_four, grad_blocks, hidden_three, gain_rows[3], ff_b, kept_b, ()
    )
    attn_full = in_order(grad_three.astype(BF))
    near, far = down(kept_b, ff_b)
    far_sum = (far[0] + swap(far[1]).astype(F32)).astype(BF)
    grad_attended = to_heads(w_attn, attn_full).astype(BF)
    grad_attended, near, far_sum = lax.optimization_barrier((grad_attended, near, far_sum))
    grad_qkv = attend_back(doc_start, cosine, sine, query, keys, values, logs, grad_attended)
    grad_qkv, far_sum, sum_dn_b = lax.optimization_barrier((grad_qkv, flip_x(far_sum), sum_dn_b))
    hidden_four = hidden_three + (near[0] + swap(near[1]).astype(F32) + far_sum.astype(F32))
    output = ring_order(hidden_four.astype(BF), 1, back=True)[None]
    grad_third = from_heads(jnp.concatenate(grad_qkv, axis=0), w_qkv)
    sum_second = ring_sum(second_grads(third_full, grad_qkv, attn_full, attended))
    grad_two, gain_grad_two = norm_back(grad_third, hidden_two, gain_rows[2], grad_three)

    grad_one, gain_grad_one, sum_gu_a, sum_dn_a, (sum_gu_b,) = feed_back(
        grad_two,
        (grad_two.astype(BF),),
        hidden_one,
        gain_rows[1],
        ff_a,
        kept_a,
        (sum_gu_b,),
    )
    conv_full = in_order(grad_one.astype(BF))
    conv_full, sum_dn_a, sum_second = lax.optimization_barrier((conv_full, sum_dn_a, sum_second))
    grad_conv = dot_nn(conv_full, w_out)
    grad_mixed, grad_kernel = conv_pull(grad_conv)
    grad_mixed = [g.astype(BF) for g in grad_mixed]
    own_first = sum(dot_nt(own_half(g), w) for g, w in zip(grad_mixed, w_in))
    other_first = sum(dot_nt(other_half(g), w) for g, w in zip(grad_mixed, w_in))
    grad_first = own_first + swap(other_first.astype(BF)).astype(F32)
    grad_zero, gain_grad_zero = norm_back(grad_first, hidden_zero, gain_rows[0], grad_one)

    grad_input = ring_order(grad_zero, 1, back=True)[None]

    kernel_full = lax.dynamic_update_slice(
        jnp.zeros((3, width), F32), grad_kernel, (0, rank * conv_cols)
    )
    small = jnp.concatenate(
        [
            jnp.stack([gain_grad_zero, gain_grad_one, gain_grad_two, gain_grad_three]),
            ring_order(kernel_full, 1),
            jnp.zeros((128 - 7, width), F32),
        ],
        axis=0,
    ).T.astype(BF)
    grad_first_w = first_grads(first_full, grad_mixed, conv_full, conv_low, small)
    summed_gu_b, summed_dn_b = finish_ff(sum_gu_b, sum_dn_b)
    summed_attn_w = finish(sum_second)
    summed_gu_a, summed_dn_a = finish_ff(sum_gu_a, sum_dn_a)
    summed_conv = finish(ring_sum(grad_first_w))
    summed_qkv = summed_attn_w[:, : query_cols + 2 * kv_cols]
    summed_attn = summed_attn_w[:, query_cols + 2 * kv_cols :].T
    summed_win = summed_conv[:, : 3 * conv_cols].reshape(rows, 3, conv_cols)
    summed_wout = summed_conv[:, 3 * conv_cols : 4 * conv_cols].T
    small_sum = summed_conv[:, 4 * conv_cols :]
    small_sum = (small_sum + swap(small_sum)).T
    return (
        output,
        grad_input,
        small_sum[:4],
        small_sum[4:7],
        summed_win,
        summed_wout,
        summed_gu_a,
        summed_dn_a,
        summed_qkv[:, :query_cols],
        summed_qkv[:, query_cols:].reshape(rows, 2, kv_cols),
        summed_attn,
        summed_gu_b,
        summed_dn_b,
    )


def solution(mesh):
    return jax.shard_map(
        per_device,
        mesh=mesh,
        in_specs=(
            P("dp", "tensor", None),
            P("dp", None),
            P(None, "dp"),
            P(None, "dp"),
            P("dp", None, "tensor"),
            P("tensor", "dp"),
            P("dp", None, "tensor"),
            P("tensor", "dp"),
            P("dp", "tensor"),
            P("dp", None, "tensor"),
            P("tensor", "dp"),
            P("dp", None, "tensor"),
            P("tensor", "dp"),
            P("dp", "tensor", None),
        ),
        out_specs=(
            P("dp", "tensor", None),
            P("dp", "tensor", None),
            P(None, "dp"),
            P(None, "dp"),
            P("dp", None, "tensor"),
            P("tensor", "dp"),
            P("dp", None, "tensor"),
            P("tensor", "dp"),
            P("dp", "tensor"),
            P("dp", None, "tensor"),
            P("tensor", "dp"),
            P("dp", None, "tensor"),
            P("tensor", "dp"),
        ),
        check_vma=False,
    )
```

```python
import functools
import math

import jax
import jax.numpy as jnp
from jax import lax
from jax.experimental import pallas as pl
from jax.experimental.pallas import tpu as pltpu
from jax.sharding import PartitionSpec as P

HD = 64
EPS = 1e-05
THETA = 1000000.0
SCALE = 0.125
BF = jnp.bfloat16
F32 = jnp.float32


def ring():
    count = lax.axis_size("dp") // 2
    return [0] + list(range(1, count, 2)) + list(range(count - 2, 0, -2))


def ring_groups():
    return [[2 * k + x for k in ring()] for x in range(2)]


def swap(values):
    return lax.ppermute(values, "tensor", [(0, 1), (1, 0)])


def flip_x(values):
    n = lax.axis_size("dp")
    return lax.ppermute(values, "dp", [(i, i ^ 1) for i in range(n)])


def by_x(mine, theirs, axis):
    x_bit = lax.axis_index("dp") % 2
    return jnp.concatenate(
        [jnp.where(x_bit == 0, mine, theirs), jnp.where(x_bit == 0, theirs, mine)], axis=axis
    )


def halves(values, axis):
    x_bit = lax.axis_index("dp") % 2
    left, right = jnp.split(values, 2, axis=axis)
    return jnp.where(x_bit == 0, left, right), jnp.where(x_bit == 0, right, left)


def between(mine, theirs):
    x_bit = lax.axis_index("dp") % 2
    count = lax.axis_size("dp") // 2
    mine, theirs = (v.reshape(count, -1, v.shape[1]) for v in (mine, theirs))
    pair = jnp.stack(
        [jnp.where(x_bit == 0, mine, theirs), jnp.where(x_bit == 0, theirs, mine)], axis=1
    )
    return pair.reshape(-1, mine.shape[2])


def ring_gather(pair):
    return lax.all_gather(pair, "dp", axis=0, axis_index_groups=ring_groups(), tiled=True)


def ring_sum(grad):
    return lax.psum_scatter(
        grad, "dp", scatter_dimension=0, axis_index_groups=ring_groups(), tiled=True
    )


def ring_order(values, axis, back=False):
    order = ring()
    if back:
        order = [order.index(k) for k in range(len(order))]
    size = values.shape[axis] // len(order)
    return jnp.concatenate(
        [lax.slice_in_dim(values, k * size, (k + 1) * size, axis=axis) for k in order], axis=axis
    )


def dot_nn(a, w):
    return jnp.dot(a, w, preferred_element_type=F32)


def dot_nt(a, w):
    return lax.dot_general(a, w, (((1,), (1,)), ((), ())), preferred_element_type=F32)


def dot_tn(a, b):
    return lax.dot_general(a, b, (((0,), (0,)), ((), ())), preferred_element_type=F32)


def params(steps=1):
    return pltpu.CompilerParams(
        vmem_limit_bytes=56 * 2**20, dimension_semantics=("arbitrary",) * steps
    )


def whole(array):
    return pl.BlockSpec(array.shape, lambda *_: (0, 0), pipeline_mode=pl.Buffered(1))


def column(array, cols, at):
    return pl.BlockSpec((array.shape[0], cols), lambda *_: (0, at), pipeline_mode=pl.Buffered(1))


def cost(flops, *arrays):
    return pl.CostEstimate(
        flops=flops,
        bytes_accessed=sum(a.size * a.dtype.itemsize for a in arrays),
        transcendentals=0,
    )


def split_sums(i, product, keep_ref, send_ref):
    @pl.when(i == 0)
    def _():
        keep_ref[...] = product

    @pl.when(i == 1)
    def _():
        send_ref[...] = product.astype(BF)


def dot_over_columns(left, right):
    return lax.dot_general(left, right, (((1,), (1,)), ((), ())), preferred_element_type=F32)


def pick(i, first, second, step):
    pl.when(i == 0)(lambda: step(first))
    pl.when(i == 1)(lambda: step(second))


def lit_parts(gate):
    sig = 1.0 / (1.0 + jnp.exp(-gate))
    return sig, gate * sig


def ff_ahead_kernel(h0, h1, w_both, w_down, both_ref, product_ref, keep_ref, send_ref):
    i = pl.program_id(0)
    unit = w_down.shape[1]

    def step(h):
        both = jnp.dot(h[...], w_both[...], preferred_element_type=F32)
        both_ref[...] = both.astype(BF)
        product = (lit_parts(both[:, :unit])[1] * both[:, unit:]).astype(BF)
        product_ref[...] = product
        split_sums(i, dot_over_columns(product, w_down[...]), keep_ref, send_ref)

    pick(i, h0, h1, step)


def ff_back_kernel(e0, e1, w_both, w_down, both_ref, dboth_ref, keep_ref, send_ref):
    i = pl.program_id(0)
    unit = w_down.shape[1]

    def step(e):
        grad = jnp.dot(e[...], w_down[...], preferred_element_type=F32)
        sig, lit = lit_parts(both_ref[:, :unit].astype(F32))
        dgate = (grad * both_ref[:, unit:].astype(F32) * (sig + lit - lit * sig)).astype(BF)
        dboth = jnp.concatenate([dgate, (grad * lit).astype(BF)], axis=1)
        dboth_ref[...] = dboth
        split_sums(i, dot_over_columns(dboth, w_both[...]), keep_ref, send_ref)

    pick(i, e0, e1, step)


def ff_both_kernel(
    h0, h1, e0, e1, w_both, w_down, product_ref, dboth_ref, keep_ref, send_ref, back_keep_ref, back_send_ref
):
    i = pl.program_id(0)
    unit = w_down.shape[1]

    def step(refs):
        h, e = refs
        both = jnp.dot(h[...], w_both[...], preferred_element_type=F32)
        grad = jnp.dot(e[...], w_down[...], preferred_element_type=F32)
        up = both[:, unit:]
        sig, lit = lit_parts(both[:, :unit])
        product = (lit * up).astype(BF)
        product_ref[...] = product
        dgate = (grad * up * (sig + lit - lit * sig)).astype(BF)
        dboth = jnp.concatenate([dgate, (grad * lit).astype(BF)], axis=1)
        dboth_ref[...] = dboth
        split_sums(i, dot_over_columns(dboth, w_both[...]), back_keep_ref, back_send_ref)
        split_sums(i, dot_over_columns(product, w_down[...]), keep_ref, send_ref)

    pick(i, (h0, e0), (h1, e1), step)


def ff_call(kernel, blocks, weights, unit, kept, out_cols, sums):
    rows, depth = blocks[0].shape

    def tile(cols):
        return pl.BlockSpec((rows, cols), lambda i: (i, 0))

    outs = [jax.ShapeDtypeStruct((2 * rows, cols), BF) for cols in out_cols]
    ends = [jax.ShapeDtypeStruct((rows, depth), kind) for kind in (F32, BF)] * sums
    return pl.pallas_call(
        kernel,
        grid=(2,),
        out_shape=[*outs, *ends],
        in_specs=[whole(b) for b in blocks]
        + [column(weights, 2 * unit, 0), column(weights, unit, 2)]
        + [tile(k.shape[1]) for k in kept],
        out_specs=[tile(cols) for cols in out_cols] + [pl.BlockSpec((rows, depth), lambda i: (0, 0))] * len(ends),
        compiler_params=params(),
        cost_estimate=cost(6 * len(blocks) * rows * depth * unit, *blocks, *kept, *outs, *ends, weights),
    )(*blocks, weights, weights, *kept)


def ff_ahead(h0, h1, weights, unit):
    both, product, *sums = ff_call(ff_ahead_kernel, (h0, h1), weights, unit, (), (2 * unit, unit), 1)
    return both, product, sums


def ff_back(e0, e1, weights, unit, both):
    dboth, *sums = ff_call(ff_back_kernel, (e0, e1), weights, unit, (both,), (2 * unit,), 1)
    return dboth, sums


def ff_both(h0, h1, e0, e1, weights, unit):
    product, dboth, *sums = ff_call(
        ff_both_kernel, (h0, h1, e0, e1), weights, unit, (), (unit, 2 * unit), 2
    )
    return product, dboth, sums[:2], sums[2:]


def weight_grad_kernel(l0, l1, l2, l3, near, far, out_ref):
    rows = l0.shape[0]
    total = jnp.dot(l0[...].T, near[:rows], preferred_element_type=F32)
    total += jnp.dot(l1[...].T, near[rows:], preferred_element_type=F32)
    total += jnp.dot(l2[...].T, far[:rows], preferred_element_type=F32)
    total += jnp.dot(l3[...].T, far[rows:], preferred_element_type=F32)
    out_ref[...] = total.astype(BF)


def weight_grad(left, near, far):
    rows, depth = left[0].shape
    tile = 256
    cols = near.shape[1]
    out = jax.ShapeDtypeStruct((depth, cols), BF)
    return pl.pallas_call(
        weight_grad_kernel,
        grid=(depth // tile,),
        out_shape=out,
        in_specs=[pl.BlockSpec((rows, tile), lambda i: (0, i))] * 4 + [whole(near), whole(far)],
        out_specs=pl.BlockSpec((tile, cols), lambda i: (i, 0)),
        compiler_params=params(),
        cost_estimate=cost(8 * rows * depth * cols, *left, near, far, out),
    )(*left, near, far)


def turn_heads(values, cosine, sine):
    half = HD // 2
    first, second = values[:half], values[half:]
    return jnp.concatenate([first * cosine - second * sine, second * cosine + first * sine], axis=0)


def allowed_keys(start_ref, begin, stop):
    shape = (stop, stop - begin)
    key = lax.broadcasted_iota(jnp.int32, shape, 0)
    query = begin + lax.broadcasted_iota(jnp.int32, shape, 1)
    return (key <= query) & (key >= start_ref[:, begin:stop])


def attend_kernel(block, start_ref, cos_ref, sin_ref, q_ref, k_ref, v_ref, qr_ref, kr_ref, vr_ref, o_ref, log_ref):
    length = q_ref.shape[1]
    cosine, sine = cos_ref[...], sin_ref[...]
    keys = turn_heads(k_ref[...], cosine, sine).astype(BF)
    values = v_ref[...].astype(BF)
    kr_ref[...] = keys
    vr_ref[...] = values
    keys_down = keys.T
    for g in range(q_ref.shape[0] // HD):
        head = slice(g * HD, (g + 1) * HD)
        query = turn_heads(q_ref[head, :], cosine, sine).astype(BF) * jnp.asarray(SCALE, BF)
        qr_ref[head, :] = query
        for begin in range(0, length, block):
            stop = begin + block
            scores = jnp.dot(keys_down[:stop], query[:, begin:stop], preferred_element_type=F32)
            scores = jnp.where(allowed_keys(start_ref, begin, stop), scores, -1e30)
            top = jnp.max(scores, axis=0, keepdims=True)
            lifted = jnp.exp(scores - top)
            total = jnp.sum(lifted, axis=0, keepdims=True)
            probs = (lifted * (1.0 / total)).astype(BF)
            out = jnp.dot(values[:, :stop], probs, preferred_element_type=F32)
            o_ref[head, begin:stop] = out.astype(BF)
            log_ref[0, g : g + 1, begin:stop] = top + jnp.log(total)


def attend(start, cosine, sine, qkv, query_rows, kv_rows):
    length = qkv.shape[1]
    heads = kv_rows // HD
    group = query_rows // heads
    q_spec = pl.BlockSpec((group, length), lambda h: (h, 0))
    out_spec = pl.BlockSpec((HD, length), lambda h: (h, 0))
    k_at, v_at = query_rows // HD, (query_rows + kv_rows) // HD
    q_out = jax.ShapeDtypeStruct((query_rows, length), BF)
    kv_out = jax.ShapeDtypeStruct((kv_rows, length), BF)
    return pl.pallas_call(
        functools.partial(attend_kernel, min(256, length)),
        grid=(heads,),
        out_shape=(q_out, kv_out, kv_out, q_out, jax.ShapeDtypeStruct((heads, group // HD, length), F32)),
        in_specs=[
            whole(start),
            whole(cosine),
            whole(sine),
            q_spec,
            pl.BlockSpec((HD, length), lambda h: (k_at + h, 0)),
            pl.BlockSpec((HD, length), lambda h: (v_at + h, 0)),
        ],
        out_specs=(
            q_spec,
            out_spec,
            out_spec,
            q_spec,
            pl.BlockSpec((1, group // HD, length), lambda h: (h, 0, 0)),
        ),
        compiler_params=params(),
        cost_estimate=cost(2 * query_rows * length * length, qkv, qkv),
    )(start, cosine, sine, qkv, qkv, qkv)


def attend_back_kernel(
    block, start_ref, cos_ref, sin_ref, q_ref, k_ref, v_ref, log_ref, do_ref, dq_ref, dk_ref, dv_ref, dk_sum, dv_sum
):
    length = q_ref.shape[1]
    cosine, sine = cos_ref[...], sin_ref[...]
    keys = k_ref[...]
    keys_down = keys.T
    values_down = v_ref[...].T
    dk_sum[...] = jnp.zeros_like(dk_sum)
    dv_sum[...] = jnp.zeros_like(dv_sum)
    over_rows = (((1,), (1,)), ((), ()))
    for g in range(q_ref.shape[0] // HD):
        head = slice(g * HD, (g + 1) * HD)
        parts = []
        for begin in range(0, length, block):
            stop = begin + block
            query = q_ref[head, begin:stop]
            grad = do_ref[head, begin:stop]
            scores = jnp.dot(keys_down[:stop], query, preferred_element_type=F32)
            scores = jnp.where(allowed_keys(start_ref, begin, stop), scores, -1e30)
            probs = jnp.exp(scores - log_ref[0, g : g + 1, begin:stop])
            grad_probs = jnp.dot(values_down[:stop], grad, preferred_element_type=F32)
            inner = jnp.sum(probs * grad_probs, axis=0, keepdims=True)
            grad_scores = (probs * (grad_probs - inner)).astype(BF)
            parts.append(jnp.dot(keys[:, :stop], grad_scores, preferred_element_type=F32))
            dk_sum[:, :stop] += lax.dot_general(query, grad_scores, over_rows, preferred_element_type=F32)
            dv_sum[:, :stop] += lax.dot_general(grad, probs.astype(BF), over_rows, preferred_element_type=F32)
        whole_head = SCALE * jnp.concatenate(parts, axis=1)
        dq_ref[head, :] = turn_heads(whole_head, cosine, -sine).astype(BF)
    dk_ref[...] = turn_heads(dk_sum[...], cosine, -sine).astype(BF)
    dv_ref[...] = dv_sum[...].astype(BF)


def attend_back(start, cosine, sine, query, keys, values, logs, grad):
    query_rows, length = query.shape
    kv_rows = keys.shape[0]
    heads = kv_rows // HD
    group = query_rows // heads
    q_spec = pl.BlockSpec((group, length), lambda h: (h, 0))
    kv_spec = pl.BlockSpec((HD, length), lambda h: (h, 0))
    q_out = jax.ShapeDtypeStruct((query_rows, length), BF)
    kv_out = jax.ShapeDtypeStruct((kv_rows, length), BF)
    return pl.pallas_call(
        functools.partial(attend_back_kernel, min(256, length)),
        grid=(heads,),
        out_shape=(q_out, kv_out, kv_out),
        in_specs=[
            whole(start),
            whole(cosine),
            whole(sine),
            q_spec,
            kv_spec,
            kv_spec,
            pl.BlockSpec((1, group // HD, length), lambda h: (h, 0, 0)),
            q_spec,
        ],
        out_specs=(q_spec, kv_spec, kv_spec),
        scratch_shapes=[pltpu.VMEM((HD, length), F32), pltpu.VMEM((HD, length), F32)],
        compiler_params=params(),
        cost_estimate=cost(6 * query_rows * length * length, query, query, grad, grad),
    )(start, cosine, sine, query, keys, values, logs, grad)


def second_grads_kernel(count, *refs):
    left0, left1, rights, out_ref = refs[0], refs[1], refs[2:-1], refs[-1]
    over_rows = (((1,), (1,)), ((), ()))
    turned = left0[...].T, left1[...].T
    at = 0
    for k, right in enumerate(rights):
        got = lax.dot_general(turned[k >= count], right[...], over_rows, preferred_element_type=F32)
        out_ref[:, at : at + got.shape[1]] = got.astype(BF)
        at += got.shape[1]


def second_grads(left0, rights0, left1, right1):
    length, depth = left0.shape
    tile = 256
    rights = [*rights0, right1]
    cols = sum(r.shape[0] for r in rights)
    out = jax.ShapeDtypeStruct((depth, cols), BF)
    left = pl.BlockSpec((length, tile), lambda i: (0, i))
    return pl.pallas_call(
        functools.partial(second_grads_kernel, len(rights0)),
        grid=(depth // tile,),
        out_shape=out,
        in_specs=[left, left] + [whole(r) for r in rights],
        out_specs=pl.BlockSpec((tile, cols), lambda i: (i, 0)),
        compiler_params=params(),
        cost_estimate=cost(2 * length * depth * cols, left0, left1, *rights, out),
    )(left0, left1, *rights)


def first_grads_kernel(left0, left1, g0, g1, g2, low, small, out_ref):
    cols = g0.shape[1]
    turned = left0[...].T
    for k, right in enumerate((g0, g1, g2)):
        got = jnp.dot(turned, right[...], preferred_element_type=F32)
        out_ref[:, k * cols : (k + 1) * cols] = got.astype(BF)
    got = jnp.dot(left1[...].T, low[...], preferred_element_type=F32)
    out_ref[:, 3 * cols : 4 * cols] = got.astype(BF)
    out_ref[:, 4 * cols :] = small[...]


def first_grads(left0, rights, left1, low, small):
    length, depth = left0.shape
    tile = 256
    cols = low.shape[1]
    width = 4 * cols + small.shape[1]
    out = jax.ShapeDtypeStruct((depth, width), BF)
    left = pl.BlockSpec((length, tile), lambda i: (0, i))
    return pl.pallas_call(
        first_grads_kernel,
        grid=(depth // tile,),
        out_shape=out,
        in_specs=[left, left]
        + [whole(r) for r in (*rights, low)]
        + [pl.BlockSpec((tile, small.shape[1]), lambda i: (i, 0))],
        out_specs=pl.BlockSpec((tile, width), lambda i: (i, 0)),
        compiler_params=params(),
        cost_estimate=cost(8 * length * depth * cols, left0, left1, *rights, low, out),
    )(left0, left1, *rights, low, small)


def inv_rms(values):
    return lax.rsqrt(jnp.mean(values * values, axis=-1, keepdims=True) + EPS)


def norm_low(values, gain):
    return (values * inv_rms(values) * gain).astype(BF)


def norm_back(grad_normed, values, gain, grad_out):
    q = inv_rms(values)
    grad_gain = jnp.sum(grad_normed * values * q, axis=0)
    a2 = grad_normed * gain
    inner = jnp.mean(a2 * values, axis=-1, keepdims=True)
    return grad_out + q * a2 - values * (q * q * q * inner), grad_gain


def rope_tables(positions):
    half = HD // 2
    freq = jnp.exp(jnp.arange(half, dtype=F32) * (-2.0 * math.log(THETA) / (2 * half)))
    angle = freq[:, None] * positions[None, :]
    return jnp.cos(angle), jnp.sin(angle)


def conv_mix(mixed, kernel, same_one, same_two):
    driven = mixed[0] * mixed[2]
    zero = jnp.zeros((2, driven.shape[1]), driven.dtype)
    back_one = jnp.concatenate([zero[:1], driven[:-1]], axis=0) * same_one
    back_two = jnp.concatenate([zero, driven[:-2]], axis=0) * same_two
    return mixed[1] * (kernel[0] * driven + kernel[1] * back_one + kernel[2] * back_two)


def per_device(
    tokens_in,
    segments,
    gains,
    taps,
    in_proj,
    out_proj,
    gate_up_a,
    down_a,
    query_w,
    key_value_w,
    attn_out_w,
    gate_up_b,
    down_b,
    cotangent,
):
    half = tokens_in.shape[1]
    segment_ids = segments[0]
    length = segment_ids.shape[0]
    rows = in_proj.shape[0]
    width = rows * lax.axis_size("dp")
    rank = lax.axis_index("tensor")

    def in_order(own):
        other = swap(own)
        first = jnp.where(rank == 0, own, other)
        second = jnp.where(rank == 0, other, own)
        return jnp.concatenate([first, second], axis=0)

    def own_half(full):
        return lax.dynamic_slice_in_dim(full, rank * half, half, 0)

    def other_half(full):
        return lax.dynamic_slice_in_dim(full, (1 - rank) * half, half, 0)

    def four(own):
        far = flip_x(own)
        return own, swap(own), far, swap(far)

    def four_back(near, far):
        far_sum = (far[0] + swap(far[1]).astype(F32)).astype(BF)
        return near[0] + swap(near[1]).astype(F32) + flip_x(far_sum).astype(F32)

    misc = jnp.concatenate(
        [gains.T, taps.T, jnp.zeros((rows, 128 - gains.shape[0] - taps.shape[0]), BF)], axis=1
    )
    conv_cols = in_proj.shape[2]
    query_cols = query_w.shape[1]
    kv_cols = key_value_w.shape[2]
    unit = down_a.shape[0] // 2

    def shared(gate_up, down):
        parts = [halves(v, 1) for v in (gate_up[:, 0], gate_up[:, 1], down.T)]
        mine = jnp.concatenate([p[0] for p in parts], axis=1)
        return by_x(mine, flip_x(jnp.concatenate([p[1] for p in parts], axis=1)), 0)

    own = jnp.concatenate([misc, in_proj[:, 0], in_proj[:, 1], in_proj[:, 2], out_proj.T], axis=1)
    conv_w = ring_gather(own)
    in_w, w_out = conv_w[:, : 128 + 3 * conv_cols], conv_w[:, 128 + 3 * conv_cols :]
    ff_a = ring_gather(shared(gate_up_a, down_a))
    own = jnp.concatenate(
        [query_w, key_value_w[:, 0], key_value_w[:, 1], attn_out_w.T], axis=1
    )
    attn_pair, ff_b_pair = by_x(own, flip_x(own), 0), shared(gate_up_b, down_b)
    attn_w = ring_gather(attn_pair)
    ff_b = ring_gather(ff_b_pair)
    sent, _, _ = lax.optimization_barrier((in_w, attn_pair, ff_b_pair))
    in_other = flip_x(sent)
    sent, in_other = lax.optimization_barrier((w_out, in_other))
    in_w = between(in_w, in_other)
    out_other = flip_x(sent)
    w_qkv = attn_w[:, : query_cols + 2 * kv_cols]
    w_attn = attn_w[:, query_cols + 2 * kv_cols :]
    w_in = [in_w[:, 128 + k * conv_cols : 128 + (k + 1) * conv_cols] for k in range(3)]
    misc_all = in_w[:, :128]

    gain_rows = misc_all[:, :4].T.astype(F32)
    taps_all = ring_order(misc_all[:, 4:7].T, 1, back=True).astype(F32)
    kernel = lax.dynamic_slice_in_dim(taps_all, rank * conv_cols, conv_cols, 1)

    index = jnp.arange(length)
    first_of_doc = jnp.sum((segment_ids[None, :] < segment_ids[:, None]).astype(jnp.int32), axis=1)
    positions = (index - first_of_doc).astype(F32)
    same_one = (positions >= 1).astype(F32)[:, None]
    same_two = (positions >= 2).astype(F32)[:, None]
    cosine, sine = rope_tables(positions)
    doc_start = first_of_doc[None, :]

    hidden_zero = ring_order(tokens_in[0], 1).astype(F32)
    first_full = in_order(norm_low(hidden_zero, gain_rows[0]))
    mixed = [dot_nn(first_full, w) for w in w_in]
    conv_out, conv_pull = jax.vjp(
        lambda mixed_in, kernel_in: conv_mix(mixed_in, kernel_in, same_one, same_two), mixed, kernel
    )
    conv_low, out_other = lax.optimization_barrier((conv_out.astype(BF), out_other))
    w_out = between(w_out, out_other)

    def collect(own, other, w):
        sent = swap(dot_nt(other, w).astype(BF))
        return dot_nt(own, w) + sent.astype(F32)

    hidden_one = hidden_zero + collect(own_half(conv_low), other_half(conv_low), w_out)

    def feed_forward(hidden, gain, weights):
        own = norm_low(hidden, gain)
        sibling, across = swap(own), flip_x(own)
        near = ff_ahead(own, sibling, weights, unit)
        near, across = lax.optimization_barrier((near, across))
        blocks = own, sibling, across, swap(across)
        far = ff_ahead(*blocks[2:], weights, unit)
        return hidden + four_back(near[2], far[2]), (blocks, near, far)

    def feed_back(grad_out, hidden, gain, weights, kept, settle):
        blocks, near, far = kept
        own = grad_out.astype(BF)
        sibling, across = swap(own), flip_x(own)
        near_back, near_sum = ff_back(own, sibling, weights, unit, near[0])
        near_sum, across, settle = lax.optimization_barrier((near_sum, across, settle))
        far_in = across, swap(across)
        g_down = weight_grad([own, sibling, *far_in], near[1], far[1])
        far_in, g_down = lax.optimization_barrier((far_in, g_down))
        far_back, far_sum = ff_back(*far_in, weights, unit, far[0])
        g_gate_up = weight_grad(blocks, near_back, far_back)
        grad_normed = four_back(near_sum, far_sum)
        grad_normed, g_gate_up = lax.optimization_barrier((grad_normed, g_gate_up))
        grad_hidden, grad_gain = norm_back(grad_normed, hidden, gain, grad_out)
        return grad_hidden, grad_gain, ring_sum(g_gate_up), ring_sum(g_down), settle

    def feed_both(hidden, gain, weights, grad_out, grads):
        own = norm_low(hidden, gain)
        sibling, across = swap(own), flip_x(own)
        near, near_back, near_down, near_sum = ff_both(own, sibling, *grads[:2], weights, unit)
        near_sum, across, grads_across = lax.optimization_barrier((near_sum, across, grads[2]))
        grads = [*grads[:2], grads_across, swap(grads_across)]
        blocks = own, sibling, across, swap(across)
        far, far_back, far_down, far_sum = ff_both(*blocks[2:], *grads[2:], weights, unit)
        g_down = weight_grad(grads, near, far)
        g_gate_up = weight_grad(blocks, near_back, far_back)
        grad_normed = four_back(near_sum, far_sum)
        grad_normed, g_gate_up = lax.optimization_barrier((grad_normed, g_gate_up))
        grad_hidden, grad_gain = norm_back(grad_normed, hidden, gain, grad_out)
        return grad_hidden, grad_gain, ring_sum(g_gate_up), ring_sum(g_down), near_down, far_down

    def finish_shared(summed):
        mine, theirs = halves(summed, 0)
        return mine.astype(F32), flip_x(theirs).astype(F32)

    def finish(summed):
        mine, theirs = halves(summed, 0)
        return mine.astype(F32) + flip_x(theirs).astype(F32)

    def finish_ff(g_gate_up, g_down):
        down = finish_shared(g_down)
        mine, theirs = finish_shared(g_gate_up)
        gate = by_x(mine[:, :unit], theirs[:, :unit], 1)
        up = by_x(mine[:, unit:], theirs[:, unit:], 1)
        return jnp.stack([gate, up], axis=1), by_x(*down, 1).T

    hidden_two, kept_a = feed_forward(hidden_one, gain_rows[1], ff_a)

    def my_part(full, other=False):
        start = (1 - rank if other else rank) * half
        return lax.dynamic_slice_in_dim(full, start, half, 1)

    def from_heads(full, w):
        over = (((0,), (1,)), ((), ()))
        sent = lax.dot_general(my_part(full, True), w, over, preferred_element_type=F32).astype(BF)
        kept = lax.dot_general(my_part(full), w, over, preferred_element_type=F32)
        return kept + swap(sent).astype(F32)

    def to_heads(w, full):
        return lax.dot_general(w, full, (((0,), (1,)), ((), ())), preferred_element_type=F32)

    third_full = in_order(norm_low(hidden_two, gain_rows[2]))
    qkv = to_heads(w_qkv, third_full)
    grad_own, hidden_two = lax.optimization_barrier((ring_order(cotangent[0], 1), hidden_two))
    grad_blocks = [grad_own, swap(grad_own), flip_x(grad_own)]
    query, keys, values, attended, logs = attend(doc_start, cosine, sine, qkv, query_cols, kv_cols)
    attended, grad_blocks = lax.optimization_barrier((attended, grad_blocks))
    hidden_three = hidden_two + from_heads(attended, w_attn)

    grad_four = ring_order(cotangent[0], 1).astype(F32)
    grad_three, gain_grad_three, sum_gu_b, sum_dn_b, near, far = feed_both(
        hidden_three, gain_rows[3], ff_b, grad_four, grad_blocks
    )
    attn_full = in_order(grad_three.astype(BF))
    far_sum = (far[0] + swap(far[1]).astype(F32)).astype(BF)
    grad_attended = to_heads(w_attn, attn_full).astype(BF)
    grad_attended, near, far_sum = lax.optimization_barrier((grad_attended, near, far_sum))
    grad_qkv = attend_back(doc_start, cosine, sine, query, keys, values, logs, grad_attended)
    grad_qkv, far_sum, sum_dn_b = lax.optimization_barrier((grad_qkv, flip_x(far_sum), sum_dn_b))
    hidden_four = hidden_three + (near[0] + swap(near[1]).astype(F32) + far_sum.astype(F32))
    output = ring_order(hidden_four.astype(BF), 1, back=True)[None]
    grad_third = from_heads(jnp.concatenate(grad_qkv, axis=0), w_qkv)
    sum_second = ring_sum(second_grads(third_full, grad_qkv, attn_full, attended))
    grad_two, gain_grad_two = norm_back(grad_third, hidden_two, gain_rows[2], grad_three)

    grad_one, gain_grad_one, sum_gu_a, sum_dn_a, (sum_gu_b,) = feed_back(
        grad_two,
        hidden_one,
        gain_rows[1],
        ff_a,
        kept_a,
        (sum_gu_b,),
    )
    conv_full = in_order(grad_one.astype(BF))
    conv_full, sum_second = lax.optimization_barrier((conv_full, sum_second))
    grad_conv = dot_nn(conv_full, w_out)
    grad_mixed, grad_kernel = conv_pull(grad_conv)
    grad_mixed = [g.astype(BF) for g in grad_mixed]
    grad_mixed, sum_dn_a = lax.optimization_barrier((grad_mixed, sum_dn_a))
    own_first = sum(dot_nt(own_half(g), w) for g, w in zip(grad_mixed, w_in))
    other_first = sum(dot_nt(other_half(g), w) for g, w in zip(grad_mixed, w_in))
    grad_first = own_first + swap(other_first.astype(BF)).astype(F32)
    grad_zero, gain_grad_zero = norm_back(grad_first, hidden_zero, gain_rows[0], grad_one)

    grad_input = ring_order(grad_zero, 1, back=True)[None]

    kernel_full = lax.dynamic_update_slice(
        jnp.zeros((3, width), F32), grad_kernel, (0, rank * conv_cols)
    )
    small = jnp.concatenate(
        [
            jnp.stack([gain_grad_zero, gain_grad_one, gain_grad_two, gain_grad_three]),
            ring_order(kernel_full, 1),
            jnp.zeros((128 - 7, width), F32),
        ],
        axis=0,
    ).T.astype(BF)
    grad_first_w = first_grads(first_full, grad_mixed, conv_full, conv_low, small)
    summed_gu_b, summed_dn_b = finish_ff(sum_gu_b, sum_dn_b)
    summed_attn_w = finish(sum_second)
    summed_gu_a, summed_dn_a = finish_ff(sum_gu_a, sum_dn_a)
    summed_conv = finish(ring_sum(grad_first_w))
    summed_qkv = summed_attn_w[:, : query_cols + 2 * kv_cols]
    summed_attn = summed_attn_w[:, query_cols + 2 * kv_cols :].T
    summed_win = summed_conv[:, : 3 * conv_cols].reshape(rows, 3, conv_cols)
    summed_wout = summed_conv[:, 3 * conv_cols : 4 * conv_cols].T
    small_sum = summed_conv[:, 4 * conv_cols :]
    small_sum = (small_sum + swap(small_sum)).T
    return (
        output,
        grad_input,
        small_sum[:4],
        small_sum[4:7],
        summed_win,
        summed_wout,
        summed_gu_a,
        summed_dn_a,
        summed_qkv[:, :query_cols],
        summed_qkv[:, query_cols:].reshape(rows, 2, kv_cols),
        summed_attn,
        summed_gu_b,
        summed_dn_b,
    )


def solution(mesh):
    return jax.shard_map(
        per_device,
        mesh=mesh,
        in_specs=(
            P("dp", "tensor", None),
            P("dp", None),
            P(None, "dp"),
            P(None, "dp"),
            P("dp", None, "tensor"),
            P("tensor", "dp"),
            P("dp", None, "tensor"),
            P("tensor", "dp"),
            P("dp", "tensor"),
            P("dp", None, "tensor"),
            P("tensor", "dp"),
            P("dp", None, "tensor"),
            P("tensor", "dp"),
            P("dp", "tensor", None),
        ),
        out_specs=(
            P("dp", "tensor", None),
            P("dp", "tensor", None),
            P(None, "dp"),
            P(None, "dp"),
            P("dp", None, "tensor"),
            P("tensor", "dp"),
            P("dp", None, "tensor"),
            P("tensor", "dp"),
            P("dp", "tensor"),
            P("dp", None, "tensor"),
            P("tensor", "dp"),
            P("dp", None, "tensor"),
            P("tensor", "dp"),
        ),
        check_vma=False,
    )
```

```python
import functools
import math

import jax
import jax.numpy as jnp
from jax import lax
from jax.experimental import pallas as pl
from jax.experimental.pallas import tpu as pltpu
from jax.sharding import PartitionSpec as P

HD = 64
EPS = 1e-05
THETA = 1000000.0
SCALE = 0.125
BF = jnp.bfloat16
F32 = jnp.float32


def ring():
    count = lax.axis_size("dp") // 2
    return [0] + list(range(1, count, 2)) + list(range(count - 2, 0, -2))


def ring_groups():
    return [[2 * k + x for k in ring()] for x in range(2)]


def swap(values):
    return lax.ppermute(values, "tensor", [(0, 1), (1, 0)])


def flip_x(values):
    n = lax.axis_size("dp")
    return lax.ppermute(values, "dp", [(i, i ^ 1) for i in range(n)])


def by_x(mine, theirs, axis):
    x_bit = lax.axis_index("dp") % 2
    return jnp.concatenate(
        [jnp.where(x_bit == 0, mine, theirs), jnp.where(x_bit == 0, theirs, mine)], axis=axis
    )


def halves(values, axis):
    x_bit = lax.axis_index("dp") % 2
    left, right = jnp.split(values, 2, axis=axis)
    return jnp.where(x_bit == 0, left, right), jnp.where(x_bit == 0, right, left)


def between(mine, theirs):
    x_bit = lax.axis_index("dp") % 2
    count = lax.axis_size("dp") // 2
    mine, theirs = (v.reshape(count, -1, v.shape[1]) for v in (mine, theirs))
    pair = jnp.stack(
        [jnp.where(x_bit == 0, mine, theirs), jnp.where(x_bit == 0, theirs, mine)], axis=1
    )
    return pair.reshape(-1, mine.shape[2])


def ring_gather(pair):
    return lax.all_gather(pair, "dp", axis=0, axis_index_groups=ring_groups(), tiled=True)


def ring_sum(grad):
    return lax.psum_scatter(
        grad, "dp", scatter_dimension=0, axis_index_groups=ring_groups(), tiled=True
    )


def ring_order(values, axis, back=False):
    order = ring()
    if back:
        order = [order.index(k) for k in range(len(order))]
    size = values.shape[axis] // len(order)
    return jnp.concatenate(
        [lax.slice_in_dim(values, k * size, (k + 1) * size, axis=axis) for k in order], axis=axis
    )


def dot_nn(a, w):
    return jnp.dot(a, w, preferred_element_type=F32)


def dot_nt(a, w):
    return lax.dot_general(a, w, (((1,), (1,)), ((), ())), preferred_element_type=F32)


def dot_tn(a, b):
    return lax.dot_general(a, b, (((0,), (0,)), ((), ())), preferred_element_type=F32)


def params(steps=1):
    return pltpu.CompilerParams(
        vmem_limit_bytes=56 * 2**20, dimension_semantics=("arbitrary",) * steps
    )


def whole(array):
    return pl.BlockSpec(array.shape, lambda *_: (0, 0), pipeline_mode=pl.Buffered(1))


def column(array, cols, at):
    return pl.BlockSpec((array.shape[0], cols), lambda *_: (0, at), pipeline_mode=pl.Buffered(1))


def cost(flops, *arrays):
    return pl.CostEstimate(
        flops=flops,
        bytes_accessed=sum(a.size * a.dtype.itemsize for a in arrays),
        transcendentals=0,
    )


def split_sums(i, product, keep_ref, send_ref):
    @pl.when(i == 0)
    def _():
        keep_ref[...] = product

    @pl.when(i == 1)
    def _():
        send_ref[...] = product.astype(BF)


def dot_over_columns(left, right):
    return lax.dot_general(left, right, (((1,), (1,)), ((), ())), preferred_element_type=F32)


def pick(i, first, second, step):
    pl.when(i == 0)(lambda: step(first))
    pl.when(i == 1)(lambda: step(second))


def lit_parts(gate):
    sig = 1.0 / (1.0 + jnp.exp(-gate))
    return sig, gate * sig


def ff_ahead_kernel(h0, h1, w_both, w_down, both_ref, product_ref, keep_ref, send_ref):
    i = pl.program_id(0)
    unit = w_down.shape[1]

    def step(h):
        both = jnp.dot(h[...], w_both[...], preferred_element_type=F32)
        both_ref[...] = both.astype(BF)
        product = (lit_parts(both[:, :unit])[1] * both[:, unit:]).astype(BF)
        product_ref[...] = product
        split_sums(i, dot_over_columns(product, w_down[...]), keep_ref, send_ref)

    pick(i, h0, h1, step)


def ff_back_kernel(e0, e1, w_both, w_down, both_ref, dboth_ref, keep_ref, send_ref):
    i = pl.program_id(0)
    unit = w_down.shape[1]

    def step(e):
        grad = jnp.dot(e[...], w_down[...], preferred_element_type=F32)
        sig, lit = lit_parts(both_ref[:, :unit].astype(F32))
        dgate = (grad * both_ref[:, unit:].astype(F32) * (sig + lit - lit * sig)).astype(BF)
        dboth = jnp.concatenate([dgate, (grad * lit).astype(BF)], axis=1)
        dboth_ref[...] = dboth
        split_sums(i, dot_over_columns(dboth, w_both[...]), keep_ref, send_ref)

    pick(i, e0, e1, step)


def ff_both_kernel(
    h0, h1, e0, e1, w_both, w_down, product_ref, dboth_ref, keep_ref, send_ref, back_keep_ref, back_send_ref
):
    i = pl.program_id(0)
    unit = w_down.shape[1]

    def step(refs):
        h, e = refs
        both = jnp.dot(h[...], w_both[...], preferred_element_type=F32)
        grad = jnp.dot(e[...], w_down[...], preferred_element_type=F32)
        up = both[:, unit:]
        sig, lit = lit_parts(both[:, :unit])
        product = (lit * up).astype(BF)
        product_ref[...] = product
        dgate = (grad * up * (sig + lit - lit * sig)).astype(BF)
        dboth = jnp.concatenate([dgate, (grad * lit).astype(BF)], axis=1)
        dboth_ref[...] = dboth
        split_sums(i, dot_over_columns(dboth, w_both[...]), back_keep_ref, back_send_ref)
        split_sums(i, dot_over_columns(product, w_down[...]), keep_ref, send_ref)

    pick(i, (h0, e0), (h1, e1), step)


def ff_call(kernel, blocks, weights, unit, kept, out_cols, sums):
    rows, depth = blocks[0].shape

    def tile(cols):
        return pl.BlockSpec((rows, cols), lambda i: (i, 0))

    outs = [jax.ShapeDtypeStruct((2 * rows, cols), BF) for cols in out_cols]
    ends = [jax.ShapeDtypeStruct((rows, depth), kind) for kind in (F32, BF)] * sums
    return pl.pallas_call(
        kernel,
        grid=(2,),
        out_shape=[*outs, *ends],
        in_specs=[whole(b) for b in blocks]
        + [column(weights, 2 * unit, 0), column(weights, unit, 2)]
        + [tile(k.shape[1]) for k in kept],
        out_specs=[tile(cols) for cols in out_cols] + [pl.BlockSpec((rows, depth), lambda i: (0, 0))] * len(ends),
        compiler_params=params(),
        cost_estimate=cost(6 * len(blocks) * rows * depth * unit, *blocks, *kept, *outs, *ends, weights),
    )(*blocks, weights, weights, *kept)


def ff_ahead(h0, h1, weights, unit):
    both, product, *sums = ff_call(ff_ahead_kernel, (h0, h1), weights, unit, (), (2 * unit, unit), 1)
    return both, product, sums


def ff_back(e0, e1, weights, unit, both):
    dboth, *sums = ff_call(ff_back_kernel, (e0, e1), weights, unit, (both,), (2 * unit,), 1)
    return dboth, sums


def ff_both(h0, h1, e0, e1, weights, unit):
    product, dboth, *sums = ff_call(
        ff_both_kernel, (h0, h1, e0, e1), weights, unit, (), (unit, 2 * unit), 2
    )
    return product, dboth, sums[:2], sums[2:]


def weight_grad_kernel(l0, l1, l2, l3, near, far, *rest):
    out_ref = rest[-1]
    rows = l0.shape[0]
    total = jnp.dot(l0[...].T, near[:rows], preferred_element_type=F32)
    total += jnp.dot(l1[...].T, near[rows:], preferred_element_type=F32)
    total += jnp.dot(l2[...].T, far[:rows], preferred_element_type=F32)
    total += jnp.dot(l3[...].T, far[rows:], preferred_element_type=F32)
    out_ref[:, : total.shape[1]] = total.astype(BF)
    if len(rest) > 1:
        out_ref[:, total.shape[1] :] = rest[0][...]


def weight_grad(left, near, far, flops_per_term=8, beside=None):
    rows, depth = left[0].shape
    tile = 256
    cols = near.shape[1]
    more = [] if beside is None else [beside]
    width = cols + sum(m.shape[1] for m in more)
    out = jax.ShapeDtypeStruct((depth, width), BF)
    return pl.pallas_call(
        weight_grad_kernel,
        grid=(depth // tile,),
        out_shape=out,
        in_specs=[pl.BlockSpec((rows, tile), lambda i: (0, i))] * 4
        + [whole(near), whole(far)]
        + [pl.BlockSpec((tile, m.shape[1]), lambda i: (i, 0)) for m in more],
        out_specs=pl.BlockSpec((tile, width), lambda i: (i, 0)),
        compiler_params=params(),
        cost_estimate=cost(flops_per_term * rows * depth * cols, out),
    )(*left, near, far, *more)


def turn_heads(values, cosine, sine):
    half = HD // 2
    first, second = values[:half], values[half:]
    return jnp.concatenate([first * cosine - second * sine, second * cosine + first * sine], axis=0)


def allowed_keys(start_ref, begin, stop):
    shape = (stop, stop - begin)
    key = lax.broadcasted_iota(jnp.int32, shape, 0)
    query = begin + lax.broadcasted_iota(jnp.int32, shape, 1)
    return (key <= query) & (key >= start_ref[:, begin:stop])


def attend_kernel(block, start_ref, cos_ref, sin_ref, q_ref, k_ref, v_ref, qr_ref, kr_ref, vr_ref, o_ref, log_ref):
    length = q_ref.shape[1]
    cosine, sine = cos_ref[...], sin_ref[...]
    keys = turn_heads(k_ref[...], cosine, sine).astype(BF)
    values = v_ref[...].astype(BF)
    kr_ref[...] = keys
    vr_ref[...] = values
    keys_down = keys.T
    for g in range(q_ref.shape[0] // HD):
        head = slice(g * HD, (g + 1) * HD)
        query = turn_heads(q_ref[head, :], cosine, sine).astype(BF) * jnp.asarray(SCALE, BF)
        qr_ref[head, :] = query
        for begin in range(0, length, block):
            stop = begin + block
            scores = jnp.dot(keys_down[:stop], query[:, begin:stop], preferred_element_type=F32)
            scores = jnp.where(allowed_keys(start_ref, begin, stop), scores, -1e30)
            top = jnp.max(scores, axis=0, keepdims=True)
            lifted = jnp.exp(scores - top)
            total = jnp.sum(lifted, axis=0, keepdims=True)
            probs = (lifted * (1.0 / total)).astype(BF)
            out = jnp.dot(values[:, :stop], probs, preferred_element_type=F32)
            o_ref[head, begin:stop] = out.astype(BF)
            log_ref[0, g : g + 1, begin:stop] = top + jnp.log(total)


def attend(start, cosine, sine, qkv, query_rows, kv_rows):
    length = qkv.shape[1]
    heads = kv_rows // HD
    group = query_rows // heads
    q_spec = pl.BlockSpec((group, length), lambda h: (h, 0))
    out_spec = pl.BlockSpec((HD, length), lambda h: (h, 0))
    k_at, v_at = query_rows // HD, (query_rows + kv_rows) // HD
    q_out = jax.ShapeDtypeStruct((query_rows, length), BF)
    kv_out = jax.ShapeDtypeStruct((kv_rows, length), BF)
    return pl.pallas_call(
        functools.partial(attend_kernel, min(256, length)),
        grid=(heads,),
        out_shape=(q_out, kv_out, kv_out, q_out, jax.ShapeDtypeStruct((heads, group // HD, length), F32)),
        in_specs=[
            whole(start),
            whole(cosine),
            whole(sine),
            q_spec,
            pl.BlockSpec((HD, length), lambda h: (k_at + h, 0)),
            pl.BlockSpec((HD, length), lambda h: (v_at + h, 0)),
        ],
        out_specs=(
            q_spec,
            out_spec,
            out_spec,
            q_spec,
            pl.BlockSpec((1, group // HD, length), lambda h: (h, 0, 0)),
        ),
        compiler_params=params(),
        cost_estimate=cost(2 * query_rows * length * length, qkv, qkv),
    )(start, cosine, sine, qkv, qkv, qkv)


def attend_back_kernel(
    block, start_ref, cos_ref, sin_ref, q_ref, k_ref, v_ref, log_ref, do_ref, dq_ref, dk_ref, dv_ref, dk_sum, dv_sum
):
    length = q_ref.shape[1]
    cosine, sine = cos_ref[...], sin_ref[...]
    keys = k_ref[...]
    keys_down = keys.T
    values_down = v_ref[...].T
    dk_sum[...] = jnp.zeros_like(dk_sum)
    dv_sum[...] = jnp.zeros_like(dv_sum)
    over_rows = (((1,), (1,)), ((), ()))
    for g in range(q_ref.shape[0] // HD):
        head = slice(g * HD, (g + 1) * HD)
        parts = []
        for begin in range(0, length, block):
            stop = begin + block
            query = q_ref[head, begin:stop]
            grad = do_ref[head, begin:stop]
            scores = jnp.dot(keys_down[:stop], query, preferred_element_type=F32)
            scores = jnp.where(allowed_keys(start_ref, begin, stop), scores, -1e30)
            probs = jnp.exp(scores - log_ref[0, g : g + 1, begin:stop])
            grad_probs = jnp.dot(values_down[:stop], grad, preferred_element_type=F32)
            inner = jnp.sum(probs * grad_probs, axis=0, keepdims=True)
            grad_scores = (probs * (grad_probs - inner)).astype(BF)
            parts.append(jnp.dot(keys[:, :stop], grad_scores, preferred_element_type=F32))
            dk_sum[:, :stop] += lax.dot_general(query, grad_scores, over_rows, preferred_element_type=F32)
            dv_sum[:, :stop] += lax.dot_general(grad, probs.astype(BF), over_rows, preferred_element_type=F32)
        whole_head = SCALE * jnp.concatenate(parts, axis=1)
        dq_ref[head, :] = turn_heads(whole_head, cosine, -sine).astype(BF)
    dk_ref[...] = turn_heads(dk_sum[...], cosine, -sine).astype(BF)
    dv_ref[...] = dv_sum[...].astype(BF)


def attend_back(start, cosine, sine, query, keys, values, logs, grad):
    query_rows, length = query.shape
    kv_rows = keys.shape[0]
    heads = kv_rows // HD
    group = query_rows // heads
    q_spec = pl.BlockSpec((group, length), lambda h: (h, 0))
    kv_spec = pl.BlockSpec((HD, length), lambda h: (h, 0))
    q_out = jax.ShapeDtypeStruct((query_rows, length), BF)
    kv_out = jax.ShapeDtypeStruct((kv_rows, length), BF)
    return pl.pallas_call(
        functools.partial(attend_back_kernel, min(256, length)),
        grid=(heads,),
        out_shape=(q_out, kv_out, kv_out),
        in_specs=[
            whole(start),
            whole(cosine),
            whole(sine),
            q_spec,
            kv_spec,
            kv_spec,
            pl.BlockSpec((1, group // HD, length), lambda h: (h, 0, 0)),
            q_spec,
        ],
        out_specs=(q_spec, kv_spec, kv_spec),
        scratch_shapes=[pltpu.VMEM((HD, length), F32), pltpu.VMEM((HD, length), F32)],
        compiler_params=params(),
        cost_estimate=cost(6 * query_rows * length * length, query, query, grad, grad),
    )(start, cosine, sine, query, keys, values, logs, grad)


def second_grads_kernel(count, *refs):
    left0, left1, rights, out_ref = refs[0], refs[1], refs[2:-1], refs[-1]
    over_rows = (((1,), (1,)), ((), ()))
    turned = left0[...].T, left1[...].T
    at = 0
    for k, right in enumerate(rights):
        got = lax.dot_general(turned[k >= count], right[...], over_rows, preferred_element_type=F32)
        out_ref[:, at : at + got.shape[1]] = got.astype(BF)
        at += got.shape[1]


def second_grads(left0, rights0, left1, right1):
    length, depth = left0.shape
    tile = 256
    rights = [*rights0, right1]
    cols = sum(r.shape[0] for r in rights)
    out = jax.ShapeDtypeStruct((depth, cols), BF)
    left = pl.BlockSpec((length, tile), lambda i: (0, i))
    return pl.pallas_call(
        functools.partial(second_grads_kernel, len(rights0)),
        grid=(depth // tile,),
        out_shape=out,
        in_specs=[left, left] + [whole(r) for r in rights],
        out_specs=pl.BlockSpec((tile, cols), lambda i: (i, 0)),
        compiler_params=params(),
        cost_estimate=cost(2 * length * depth * cols, left0, left1, *rights, out),
    )(left0, left1, *rights)


def first_grads_kernel(left0, left1, g0, g1, g2, low, extra, out_ref):
    cols = g0.shape[1]
    turned = left0[...].T
    for k, right in enumerate((g0, g1, g2)):
        got = jnp.dot(turned, right[...], preferred_element_type=F32)
        out_ref[:, k * cols : (k + 1) * cols] = got.astype(BF)
    got = jnp.dot(left1[...].T, low[...], preferred_element_type=F32)
    out_ref[:, 3 * cols : 4 * cols] = got.astype(BF)
    out_ref[:, 4 * cols :] = extra[...]


def first_grads(left0, rights, left1, low, extra):
    length, depth = left0.shape
    tile = 256
    cols = low.shape[1]
    width = 4 * cols + extra.shape[1]
    out = jax.ShapeDtypeStruct((depth, width), BF)
    left = pl.BlockSpec((length, tile), lambda i: (0, i))
    return pl.pallas_call(
        first_grads_kernel,
        grid=(depth // tile,),
        out_shape=out,
        in_specs=[left, left]
        + [whole(r) for r in (*rights, low)]
        + [pl.BlockSpec((tile, extra.shape[1]), lambda i: (i, 0))],
        out_specs=pl.BlockSpec((tile, width), lambda i: (i, 0)),
        compiler_params=params(),
        cost_estimate=cost(8 * length * depth * cols, left0, left1, *rights, low, out),
    )(left0, left1, *rights, low, extra)


def inv_rms(values):
    return lax.rsqrt(jnp.mean(values * values, axis=-1, keepdims=True) + EPS)


def norm_low(values, gain):
    return (values * inv_rms(values) * gain).astype(BF)


def norm_back(grad_normed, values, gain, grad_out):
    q = inv_rms(values)
    grad_gain = jnp.sum(grad_normed * values * q, axis=0)
    a2 = grad_normed * gain
    inner = jnp.mean(a2 * values, axis=-1, keepdims=True)
    return grad_out + q * a2 - values * (q * q * q * inner), grad_gain


def rope_tables(positions):
    half = HD // 2
    freq = jnp.exp(jnp.arange(half, dtype=F32) * (-2.0 * math.log(THETA) / (2 * half)))
    angle = freq[:, None] * positions[None, :]
    return jnp.cos(angle), jnp.sin(angle)


def conv_mix(mixed, kernel, same_one, same_two):
    driven = mixed[0] * mixed[2]
    zero = jnp.zeros((2, driven.shape[1]), driven.dtype)
    back_one = jnp.concatenate([zero[:1], driven[:-1]], axis=0) * same_one
    back_two = jnp.concatenate([zero, driven[:-2]], axis=0) * same_two
    return mixed[1] * (kernel[0] * driven + kernel[1] * back_one + kernel[2] * back_two)


def per_device(
    tokens_in,
    segments,
    gains,
    taps,
    in_proj,
    out_proj,
    gate_up_a,
    down_a,
    query_w,
    key_value_w,
    attn_out_w,
    gate_up_b,
    down_b,
    cotangent,
):
    half = tokens_in.shape[1]
    segment_ids = segments[0]
    length = segment_ids.shape[0]
    rows = in_proj.shape[0]
    width = rows * lax.axis_size("dp")
    rank = lax.axis_index("tensor")

    def in_order(own):
        other = swap(own)
        first = jnp.where(rank == 0, own, other)
        second = jnp.where(rank == 0, other, own)
        return jnp.concatenate([first, second], axis=0)

    def own_half(full):
        return lax.dynamic_slice_in_dim(full, rank * half, half, 0)

    def other_half(full):
        return lax.dynamic_slice_in_dim(full, (1 - rank) * half, half, 0)

    def four(own):
        far = flip_x(own)
        return own, swap(own), far, swap(far)

    def far_total(far):
        return (far[0] + swap(far[1]).astype(F32)).astype(BF)

    def four_total(near, far_sum):
        return near[0] + swap(near[1]).astype(F32) + flip_x(far_sum).astype(F32)

    def four_back(near, far):
        return four_total(near, far_total(far))

    misc = jnp.concatenate(
        [gains.T, taps.T, jnp.zeros((rows, 128 - gains.shape[0] - taps.shape[0]), BF)], axis=1
    )
    conv_cols = in_proj.shape[2]
    query_cols = query_w.shape[1]
    kv_cols = key_value_w.shape[2]
    unit = down_a.shape[0] // 2

    def shared(gate_up, down):
        parts = [halves(v, 1) for v in (gate_up[:, 0], gate_up[:, 1], down.T)]
        mine = jnp.concatenate([p[0] for p in parts], axis=1)
        return by_x(mine, flip_x(jnp.concatenate([p[1] for p in parts], axis=1)), 0)

    own = jnp.concatenate([misc, in_proj[:, 0], in_proj[:, 1], in_proj[:, 2], out_proj.T], axis=1)
    conv_w = ring_gather(own)
    in_w, w_out = conv_w[:, : 128 + 3 * conv_cols], conv_w[:, 128 + 3 * conv_cols :]
    ff_a = ring_gather(shared(gate_up_a, down_a))
    own = jnp.concatenate(
        [query_w, key_value_w[:, 0], key_value_w[:, 1], attn_out_w.T], axis=1
    )
    attn_pair, ff_b_pair = by_x(own, flip_x(own), 0), shared(gate_up_b, down_b)
    attn_w = ring_gather(attn_pair)
    ff_b = ring_gather(ff_b_pair)
    sent, _, _ = lax.optimization_barrier((in_w, attn_pair, ff_b_pair))
    in_other = flip_x(sent)
    sent, in_other = lax.optimization_barrier((w_out, in_other))
    in_w = between(in_w, in_other)
    out_other = flip_x(sent)
    w_qkv = attn_w[:, : query_cols + 2 * kv_cols]
    w_attn = attn_w[:, query_cols + 2 * kv_cols :]
    w_in = [in_w[:, 128 + k * conv_cols : 128 + (k + 1) * conv_cols] for k in range(3)]
    misc_all = in_w[:, :128]

    gain_rows = misc_all[:, :4].T.astype(F32)
    taps_all = ring_order(misc_all[:, 4:7].T, 1, back=True).astype(F32)
    kernel = lax.dynamic_slice_in_dim(taps_all, rank * conv_cols, conv_cols, 1)

    index = jnp.arange(length)
    first_of_doc = jnp.sum((segment_ids[None, :] < segment_ids[:, None]).astype(jnp.int32), axis=1)
    positions = (index - first_of_doc).astype(F32)
    same_one = (positions >= 1).astype(F32)[:, None]
    same_two = (positions >= 2).astype(F32)[:, None]
    cosine, sine = rope_tables(positions)
    doc_start = first_of_doc[None, :]

    hidden_zero = ring_order(tokens_in[0], 1).astype(F32)
    first_full = in_order(norm_low(hidden_zero, gain_rows[0]))
    mixed = [dot_nn(first_full, w) for w in w_in]
    conv_out, conv_pull = jax.vjp(
        lambda mixed_in, kernel_in: conv_mix(mixed_in, kernel_in, same_one, same_two), mixed, kernel
    )
    conv_low, out_other = lax.optimization_barrier((conv_out.astype(BF), out_other))
    w_out = between(w_out, out_other)

    def collect(own, other, w):
        sent = swap(dot_nt(other, w).astype(BF))
        return dot_nt(own, w) + sent.astype(F32)

    hidden_one = hidden_zero + collect(own_half(conv_low), other_half(conv_low), w_out)

    def feed_forward(hidden, gain, weights):
        own = norm_low(hidden, gain)
        sibling, across = swap(own), flip_x(own)
        near = ff_ahead(own, sibling, weights, unit)
        near, across = lax.optimization_barrier((near, across))
        blocks = own, sibling, across, swap(across)
        far = ff_ahead(*blocks[2:], weights, unit)
        return hidden + four_back(near[2], far[2]), (blocks, near, far)

    def feed_back(grad_out, hidden, gain, weights, kept, settle, other):
        blocks, near, far = kept
        own = grad_out.astype(BF)
        sibling, across = swap(own), flip_x(own)
        near_back, near_sum = ff_back(own, sibling, weights, unit, near[0])
        inputs, near_sum = lax.optimization_barrier((other[1:], near_sum))
        other = other[0](*inputs)
        near_sum, across, settle, other = lax.optimization_barrier((near_sum, across, settle, other))
        far_in = across, swap(across)
        far_back, far_sum = ff_back(*far_in, weights, unit, far[0])
        far_sum, far_back = lax.optimization_barrier((far_total(far_sum), far_back))
        g_gate_up = weight_grad(blocks, near_back, far_back)
        product, g_gate_up = lax.optimization_barrier((near[1], g_gate_up))
        g_down = weight_grad([own, sibling, *far_in], product, far[1], 0)
        grad_normed = four_total(near_sum, far_sum)
        grad_normed, g_down = lax.optimization_barrier((grad_normed, g_down))
        grad_hidden, grad_gain = norm_back(grad_normed, hidden, gain, grad_out)
        return grad_hidden, grad_gain, ring_sum(g_gate_up), g_down, settle, ring_sum(other)

    def feed_both(hidden, gain, weights, grad_out, grads):
        own = norm_low(hidden, gain)
        sibling, across = swap(own), flip_x(own)
        near, near_back, near_down, near_sum = ff_both(own, sibling, *grads[:2], weights, unit)
        near_sum, across = lax.optimization_barrier((near_sum, across))
        blocks = own, sibling, across, swap(across)
        far, far_back, far_down, far_sum = ff_both(*blocks[2:], *grads[2:], weights, unit)
        far_sum, far = lax.optimization_barrier((far_total(far_sum), far))
        g_gate_up = weight_grad(blocks, near_back, far_back)
        near, g_gate_up = lax.optimization_barrier((near, g_gate_up))
        grad_w = weight_grad(grads, near, far, 0, g_gate_up)
        grad_normed = four_total(near_sum, far_sum)
        grad_normed, grad_w = lax.optimization_barrier((grad_normed, grad_w))
        grad_hidden, grad_gain = norm_back(grad_normed, hidden, gain, grad_out)
        sums = ring_sum(grad_w)
        return grad_hidden, grad_gain, sums, near_down, far_down

    def finish_shared(summed):
        mine, theirs = halves(summed, 0)
        return mine.astype(F32), flip_x(theirs).astype(F32)

    def finish(summed):
        mine, theirs = halves(summed, 0)
        return mine.astype(F32) + flip_x(theirs).astype(F32)

    def finish_all(summed):
        mine, theirs = finish_shared(summed)
        down, gate, up = (
            by_x(mine[:, k * unit : (k + 1) * unit], theirs[:, k * unit : (k + 1) * unit], 1)
            for k in range(3)
        )
        return jnp.stack([gate, up], axis=1), down.T

    def finish_gate_up(summed):
        mine, theirs = finish_shared(summed)
        gate = by_x(mine[:, :unit], theirs[:, :unit], 1)
        up = by_x(mine[:, unit:], theirs[:, unit:], 1)
        return jnp.stack([gate, up], axis=1)

    hidden_two, kept_a = feed_forward(hidden_one, gain_rows[1], ff_a)

    def my_part(full, other=False):
        start = (1 - rank if other else rank) * half
        return lax.dynamic_slice_in_dim(full, start, half, 1)

    def from_heads(full, w):
        over = (((0,), (1,)), ((), ()))
        sent = lax.dot_general(my_part(full, True), w, over, preferred_element_type=F32).astype(BF)
        kept = lax.dot_general(my_part(full), w, over, preferred_element_type=F32)
        return kept + swap(sent).astype(F32)

    def to_heads(w, full):
        return lax.dot_general(w, full, (((0,), (1,)), ((), ())), preferred_element_type=F32)

    third_full = in_order(norm_low(hidden_two, gain_rows[2]))
    qkv = to_heads(w_qkv, third_full)
    grad_own, hidden_two = lax.optimization_barrier((ring_order(cotangent[0], 1), hidden_two))
    grad_blocks = [grad_own, swap(grad_own), flip_x(grad_own)]
    query, keys, values, attended, logs = attend(doc_start, cosine, sine, qkv, query_cols, kv_cols)
    attended, grads_across = lax.optimization_barrier((attended, grad_blocks[2]))
    grad_blocks = [*grad_blocks[:2], grads_across, swap(grads_across)]
    hidden_three = hidden_two + from_heads(attended, w_attn)

    grad_four = ring_order(cotangent[0], 1).astype(F32)
    grad_three, gain_grad_three, sum_b, near, far = feed_both(
        hidden_three, gain_rows[3], ff_b, grad_four, grad_blocks
    )
    attn_full = in_order(grad_three.astype(BF))
    far_sum = far_total(far)
    grad_attended = to_heads(w_attn, attn_full).astype(BF)
    grad_attended, near, far_sum = lax.optimization_barrier((grad_attended, near, far_sum))
    grad_qkv = attend_back(doc_start, cosine, sine, query, keys, values, logs, grad_attended)
    grad_qkv, far_sum = lax.optimization_barrier((grad_qkv, flip_x(far_sum)))
    hidden_four = hidden_three + (near[0] + swap(near[1]).astype(F32) + far_sum.astype(F32))
    output = ring_order(hidden_four.astype(BF), 1, back=True)[None]
    grad_third = from_heads(jnp.concatenate(grad_qkv, axis=0), w_qkv)
    grad_two, gain_grad_two = norm_back(grad_third, hidden_two, gain_rows[2], grad_three)

    grad_one, gain_grad_one, sum_gu_a, g_down_a, (sum_b,), sum_second = feed_back(
        grad_two,
        hidden_one,
        gain_rows[1],
        ff_a,
        kept_a,
        (sum_b,),
        (second_grads, third_full, grad_qkv, attn_full, attended),
    )
    conv_full = in_order(grad_one.astype(BF))
    conv_full, sum_second = lax.optimization_barrier((conv_full, sum_second))
    grad_conv = dot_nn(conv_full, w_out)
    grad_mixed, grad_kernel = conv_pull(grad_conv)
    grad_mixed = [g.astype(BF) for g in grad_mixed]
    grad_first_w = first_grads(first_full, grad_mixed, conv_full, conv_low, g_down_a)
    sum_conv = ring_sum(grad_first_w)
    grad_mixed, sum_gu_a, _ = lax.optimization_barrier((grad_mixed, sum_gu_a, grad_first_w))
    own_first = sum(dot_nt(own_half(g), w) for g, w in zip(grad_mixed, w_in))
    other_first = sum(dot_nt(other_half(g), w) for g, w in zip(grad_mixed, w_in))
    grad_first = own_first + swap(other_first.astype(BF)).astype(F32)
    grad_zero, gain_grad_zero = norm_back(grad_first, hidden_zero, gain_rows[0], grad_one)

    grad_input = ring_order(grad_zero, 1, back=True)[None]

    kernel_full = lax.dynamic_update_slice(
        jnp.zeros((3, width), F32), grad_kernel, (0, rank * conv_cols)
    )
    small = jnp.concatenate(
        [
            ring_order(
                jnp.stack([gain_grad_zero, gain_grad_one, gain_grad_two, gain_grad_three]), 1, back=True
            ),
            kernel_full,
            jnp.zeros((1, width), F32),
        ],
        axis=0,
    )
    step, count = 1, lax.axis_size("dp")
    small = small + swap(small)
    while step < count:
        small = small + lax.ppermute(small, "dp", [(i, i ^ step) for i in range(count)])
        step *= 2
    small_sum = lax.dynamic_slice_in_dim(small, lax.axis_index("dp") * rows, rows, 1)
    sum_b, sum_second, sum_gu_a = lax.optimization_barrier((sum_b, sum_second, sum_gu_a))
    summed_gu_b, summed_dn_b = finish_all(sum_b)
    summed_attn_w = finish(sum_second)
    summed_gu_a = finish_gate_up(sum_gu_a)
    mine, theirs = halves(sum_conv, 0)
    mine, theirs = mine.astype(F32), flip_x(theirs).astype(F32)
    summed_conv = mine[:, : 4 * conv_cols] + theirs[:, : 4 * conv_cols]
    summed_dn_a = by_x(mine[:, 4 * conv_cols :], theirs[:, 4 * conv_cols :], 1).T
    summed_qkv = summed_attn_w[:, : query_cols + 2 * kv_cols]
    summed_attn = summed_attn_w[:, query_cols + 2 * kv_cols :].T
    summed_win = summed_conv[:, : 3 * conv_cols].reshape(rows, 3, conv_cols)
    summed_wout = summed_conv[:, 3 * conv_cols :].T
    return (
        output,
        grad_input,
        small_sum[:4],
        small_sum[4:7],
        summed_win,
        summed_wout,
        summed_gu_a,
        summed_dn_a,
        summed_qkv[:, :query_cols],
        summed_qkv[:, query_cols:].reshape(rows, 2, kv_cols),
        summed_attn,
        summed_gu_b,
        summed_dn_b,
    )


def solution(mesh):
    return jax.shard_map(
        per_device,
        mesh=mesh,
        in_specs=(
            P("dp", "tensor", None),
            P("dp", None),
            P(None, "dp"),
            P(None, "dp"),
            P("dp", None, "tensor"),
            P("tensor", "dp"),
            P("dp", None, "tensor"),
            P("tensor", "dp"),
            P("dp", "tensor"),
            P("dp", None, "tensor"),
            P("tensor", "dp"),
            P("dp", None, "tensor"),
            P("tensor", "dp"),
            P("dp", "tensor", None),
        ),
        out_specs=(
            P("dp", "tensor", None),
            P("dp", "tensor", None),
            P(None, "dp"),
            P(None, "dp"),
            P("dp", None, "tensor"),
            P("tensor", "dp"),
            P("dp", None, "tensor"),
            P("tensor", "dp"),
            P("dp", "tensor"),
            P("dp", None, "tensor"),
            P("tensor", "dp"),
            P("dp", None, "tensor"),
            P("tensor", "dp"),
        ),
        check_vma=False,
    )
```

```python
import functools
import math

import jax
import jax.numpy as jnp
from jax import lax
from jax.experimental import pallas as pl
from jax.experimental.pallas import tpu as pltpu
from jax.sharding import PartitionSpec as P

HD = 64
EPS = 1e-05
THETA = 1000000.0
SCALE = 0.125
BF = jnp.bfloat16
F32 = jnp.float32


def ring():
    count = lax.axis_size("dp") // 2
    return [0] + list(range(1, count, 2)) + list(range(count - 2, 0, -2))


def ring_groups():
    return [[2 * k + x for k in ring()] for x in range(2)]


def swap(values):
    return lax.ppermute(values, "tensor", [(0, 1), (1, 0)])


def flip_x(values):
    n = lax.axis_size("dp")
    return lax.ppermute(values, "dp", [(i, i ^ 1) for i in range(n)])


def by_x(mine, theirs, axis):
    x_bit = lax.axis_index("dp") % 2
    return jnp.concatenate(
        [jnp.where(x_bit == 0, mine, theirs), jnp.where(x_bit == 0, theirs, mine)], axis=axis
    )


def halves(values, axis):
    x_bit = lax.axis_index("dp") % 2
    left, right = jnp.split(values, 2, axis=axis)
    return jnp.where(x_bit == 0, left, right), jnp.where(x_bit == 0, right, left)


def between(mine, theirs):
    x_bit = lax.axis_index("dp") % 2
    count = lax.axis_size("dp") // 2
    mine, theirs = (v.reshape(count, -1, v.shape[1]) for v in (mine, theirs))
    pair = jnp.stack(
        [jnp.where(x_bit == 0, mine, theirs), jnp.where(x_bit == 0, theirs, mine)], axis=1
    )
    return pair.reshape(-1, mine.shape[2])


def ring_gather(pair):
    return lax.all_gather(pair, "dp", axis=0, axis_index_groups=ring_groups(), tiled=True)


def ring_sum(grad):
    return lax.psum_scatter(
        grad, "dp", scatter_dimension=0, axis_index_groups=ring_groups(), tiled=True
    )


def ring_order(values, axis, back=False):
    order = ring()
    if back:
        order = [order.index(k) for k in range(len(order))]
    size = values.shape[axis] // len(order)
    return jnp.concatenate(
        [lax.slice_in_dim(values, k * size, (k + 1) * size, axis=axis) for k in order], axis=axis
    )


def dot_nn(a, w):
    return jnp.dot(a, w, preferred_element_type=F32)


def dot_nt(a, w):
    return lax.dot_general(a, w, (((1,), (1,)), ((), ())), preferred_element_type=F32)


def dot_tn(a, b):
    return lax.dot_general(a, b, (((0,), (0,)), ((), ())), preferred_element_type=F32)


def params(steps=1):
    return pltpu.CompilerParams(
        vmem_limit_bytes=56 * 2**20, dimension_semantics=("arbitrary",) * steps
    )


def whole(array):
    return pl.BlockSpec(array.shape, lambda *_: (0, 0), pipeline_mode=pl.Buffered(1))


def column(array, cols, at):
    return pl.BlockSpec((array.shape[0], cols), lambda *_: (0, at), pipeline_mode=pl.Buffered(1))


def cost(flops, *arrays):
    return pl.CostEstimate(
        flops=flops,
        bytes_accessed=sum(a.size * a.dtype.itemsize for a in arrays),
        transcendentals=0,
    )


def split_sums(i, product, keep_ref, send_ref):
    @pl.when(i == 0)
    def _():
        keep_ref[...] = product

    @pl.when(i == 1)
    def _():
        send_ref[...] = product.astype(BF)


def dot_over_columns(left, right):
    return lax.dot_general(left, right, (((1,), (1,)), ((), ())), preferred_element_type=F32)


def pick(i, first, second, step):
    pl.when(i == 0)(lambda: step(first))
    pl.when(i == 1)(lambda: step(second))


def lit_parts(gate):
    sig = 1.0 / (1.0 + jnp.exp(-gate))
    return sig, gate * sig


def ff_ahead_kernel(h0, h1, w_both, w_down, both_ref, product_ref, keep_ref, send_ref):
    i = pl.program_id(0)
    unit = w_down.shape[1]

    def step(h):
        both = jnp.dot(h[...], w_both[...], preferred_element_type=F32)
        both_ref[...] = both.astype(BF)
        product = (lit_parts(both[:, :unit])[1] * both[:, unit:]).astype(BF)
        product_ref[...] = product
        split_sums(i, dot_over_columns(product, w_down[...]), keep_ref, send_ref)

    pick(i, h0, h1, step)


def ff_back_kernel(e0, e1, w_both, w_down, both_ref, dboth_ref, keep_ref, send_ref):
    i = pl.program_id(0)
    unit = w_down.shape[1]

    def step(e):
        grad = jnp.dot(e[...], w_down[...], preferred_element_type=F32)
        sig, lit = lit_parts(both_ref[:, :unit].astype(F32))
        dgate = (grad * both_ref[:, unit:].astype(F32) * (sig + lit - lit * sig)).astype(BF)
        dboth = jnp.concatenate([dgate, (grad * lit).astype(BF)], axis=1)
        dboth_ref[...] = dboth
        split_sums(i, dot_over_columns(dboth, w_both[...]), keep_ref, send_ref)

    pick(i, e0, e1, step)


def ff_both_kernel(
    h0, h1, e0, e1, w_both, w_down, product_ref, dboth_ref, keep_ref, send_ref, back_keep_ref, back_send_ref
):
    i = pl.program_id(0)
    unit = w_down.shape[1]

    def step(refs):
        h, e = refs
        both = jnp.dot(h[...], w_both[...], preferred_element_type=F32)
        grad = jnp.dot(e[...], w_down[...], preferred_element_type=F32)
        up = both[:, unit:]
        sig, lit = lit_parts(both[:, :unit])
        product = (lit * up).astype(BF)
        product_ref[...] = product
        dgate = (grad * up * (sig + lit - lit * sig)).astype(BF)
        dboth = jnp.concatenate([dgate, (grad * lit).astype(BF)], axis=1)
        dboth_ref[...] = dboth
        split_sums(i, dot_over_columns(dboth, w_both[...]), back_keep_ref, back_send_ref)
        split_sums(i, dot_over_columns(product, w_down[...]), keep_ref, send_ref)

    pick(i, (h0, e0), (h1, e1), step)


def ff_call(kernel, blocks, weights, unit, kept, out_cols, sums):
    rows, depth = blocks[0].shape

    def tile(cols):
        return pl.BlockSpec((rows, cols), lambda i: (i, 0))

    outs = [jax.ShapeDtypeStruct((2 * rows, cols), BF) for cols in out_cols]
    ends = [jax.ShapeDtypeStruct((rows, depth), kind) for kind in (F32, BF)] * sums
    return pl.pallas_call(
        kernel,
        grid=(2,),
        out_shape=[*outs, *ends],
        in_specs=[whole(b) for b in blocks]
        + [column(weights, 2 * unit, 0), column(weights, unit, 2)]
        + [tile(k.shape[1]) for k in kept],
        out_specs=[tile(cols) for cols in out_cols] + [pl.BlockSpec((rows, depth), lambda i: (0, 0))] * len(ends),
        compiler_params=params(),
        cost_estimate=cost(6 * len(blocks) * rows * depth * unit, *blocks, *kept, *outs, *ends, weights),
    )(*blocks, weights, weights, *kept)


def ff_ahead(h0, h1, weights, unit):
    both, product, *sums = ff_call(ff_ahead_kernel, (h0, h1), weights, unit, (), (2 * unit, unit), 1)
    return both, product, sums


def ff_back(e0, e1, weights, unit, both):
    dboth, *sums = ff_call(ff_back_kernel, (e0, e1), weights, unit, (both,), (2 * unit,), 1)
    return dboth, sums


def ff_both(h0, h1, e0, e1, weights, unit):
    product, dboth, *sums = ff_call(
        ff_both_kernel, (h0, h1, e0, e1), weights, unit, (), (unit, 2 * unit), 2
    )
    return product, dboth, sums[:2], sums[2:]


def weight_grad_kernel(l0, l1, l2, l3, near, far, *rest):
    out_ref = rest[-1]
    rows = l0.shape[0]
    total = jnp.dot(l0[...].T, near[:rows], preferred_element_type=F32)
    total += jnp.dot(l1[...].T, near[rows:], preferred_element_type=F32)
    total += jnp.dot(l2[...].T, far[:rows], preferred_element_type=F32)
    total += jnp.dot(l3[...].T, far[rows:], preferred_element_type=F32)
    out_ref[:, : total.shape[1]] = total.astype(BF)
    if len(rest) > 1:
        out_ref[:, total.shape[1] :] = rest[0][...]


def weight_grad(left, near, far, flops_per_term=8, beside=None):
    rows, depth = left[0].shape
    tile = 256
    cols = near.shape[1]
    more = [] if beside is None else [beside]
    width = cols + sum(m.shape[1] for m in more)
    out = jax.ShapeDtypeStruct((depth, width), BF)
    return pl.pallas_call(
        weight_grad_kernel,
        grid=(depth // tile,),
        out_shape=out,
        in_specs=[pl.BlockSpec((rows, tile), lambda i: (0, i))] * 4
        + [whole(near), whole(far)]
        + [pl.BlockSpec((tile, m.shape[1]), lambda i: (i, 0)) for m in more],
        out_specs=pl.BlockSpec((tile, width), lambda i: (i, 0)),
        compiler_params=params(),
        cost_estimate=cost(flops_per_term * rows * depth * cols, out),
    )(*left, near, far, *more)


def turn_heads(values, cosine, sine):
    half = HD // 2
    first, second = values[:half], values[half:]
    return jnp.concatenate([first * cosine - second * sine, second * cosine + first * sine], axis=0)


def allowed_keys(start_ref, begin, stop):
    shape = (stop, stop - begin)
    key = lax.broadcasted_iota(jnp.int32, shape, 0)
    query = begin + lax.broadcasted_iota(jnp.int32, shape, 1)
    return (key <= query) & (key >= start_ref[:, begin:stop])


def attend_kernel(block, start_ref, cos_ref, sin_ref, q_ref, k_ref, v_ref, qr_ref, kr_ref, vr_ref, o_ref, log_ref):
    length = q_ref.shape[1]
    cosine, sine = cos_ref[...], sin_ref[...]
    keys = turn_heads(k_ref[...], cosine, sine).astype(BF)
    values = v_ref[...].astype(BF)
    kr_ref[...] = keys
    vr_ref[...] = values
    keys_down = keys.T
    for g in range(q_ref.shape[0] // HD):
        head = slice(g * HD, (g + 1) * HD)
        query = turn_heads(q_ref[head, :], cosine, sine).astype(BF) * jnp.asarray(SCALE, BF)
        qr_ref[head, :] = query
        for begin in range(0, length, block):
            stop = begin + block
            scores = jnp.dot(keys_down[:stop], query[:, begin:stop], preferred_element_type=F32)
            scores = jnp.where(allowed_keys(start_ref, begin, stop), scores, -1e30)
            top = jnp.max(scores, axis=0, keepdims=True)
            lifted = jnp.exp(scores - top)
            total = jnp.sum(lifted, axis=0, keepdims=True)
            probs = (lifted * (1.0 / total)).astype(BF)
            out = jnp.dot(values[:, :stop], probs, preferred_element_type=F32)
            o_ref[head, begin:stop] = out.astype(BF)
            log_ref[0, g : g + 1, begin:stop] = top + jnp.log(total)


def attend(start, cosine, sine, qkv, query_rows, kv_rows):
    length = qkv.shape[1]
    heads = kv_rows // HD
    group = query_rows // heads
    q_spec = pl.BlockSpec((group, length), lambda h: (h, 0))
    out_spec = pl.BlockSpec((HD, length), lambda h: (h, 0))
    k_at, v_at = query_rows // HD, (query_rows + kv_rows) // HD
    q_out = jax.ShapeDtypeStruct((query_rows, length), BF)
    kv_out = jax.ShapeDtypeStruct((kv_rows, length), BF)
    return pl.pallas_call(
        functools.partial(attend_kernel, min(256, length)),
        grid=(heads,),
        out_shape=(q_out, kv_out, kv_out, q_out, jax.ShapeDtypeStruct((heads, group // HD, length), F32)),
        in_specs=[
            whole(start),
            whole(cosine),
            whole(sine),
            q_spec,
            pl.BlockSpec((HD, length), lambda h: (k_at + h, 0)),
            pl.BlockSpec((HD, length), lambda h: (v_at + h, 0)),
        ],
        out_specs=(
            q_spec,
            out_spec,
            out_spec,
            q_spec,
            pl.BlockSpec((1, group // HD, length), lambda h: (h, 0, 0)),
        ),
        compiler_params=params(),
        cost_estimate=cost(2 * query_rows * length * length, qkv, qkv),
    )(start, cosine, sine, qkv, qkv, qkv)


def attend_back_kernel(
    block, start_ref, cos_ref, sin_ref, q_ref, k_ref, v_ref, log_ref, do_ref, dq_ref, dk_ref, dv_ref, dk_sum, dv_sum
):
    length = q_ref.shape[1]
    cosine, sine = cos_ref[...], sin_ref[...]
    keys = k_ref[...]
    keys_down = keys.T
    values_down = v_ref[...].T
    dk_sum[...] = jnp.zeros_like(dk_sum)
    dv_sum[...] = jnp.zeros_like(dv_sum)
    over_rows = (((1,), (1,)), ((), ()))
    for g in range(q_ref.shape[0] // HD):
        head = slice(g * HD, (g + 1) * HD)
        parts = []
        for begin in range(0, length, block):
            stop = begin + block
            query = q_ref[head, begin:stop]
            grad = do_ref[head, begin:stop]
            scores = jnp.dot(keys_down[:stop], query, preferred_element_type=F32)
            scores = jnp.where(allowed_keys(start_ref, begin, stop), scores, -1e30)
            probs = jnp.exp(scores - log_ref[0, g : g + 1, begin:stop])
            grad_probs = jnp.dot(values_down[:stop], grad, preferred_element_type=F32)
            inner = jnp.sum(probs * grad_probs, axis=0, keepdims=True)
            grad_scores = (probs * (grad_probs - inner)).astype(BF)
            parts.append(jnp.dot(keys[:, :stop], grad_scores, preferred_element_type=F32))
            dk_sum[:, :stop] += lax.dot_general(query, grad_scores, over_rows, preferred_element_type=F32)
            dv_sum[:, :stop] += lax.dot_general(grad, probs.astype(BF), over_rows, preferred_element_type=F32)
        whole_head = SCALE * jnp.concatenate(parts, axis=1)
        dq_ref[head, :] = turn_heads(whole_head, cosine, -sine).astype(BF)
    dk_ref[...] = turn_heads(dk_sum[...], cosine, -sine).astype(BF)
    dv_ref[...] = dv_sum[...].astype(BF)


def attend_back(start, cosine, sine, query, keys, values, logs, grad):
    query_rows, length = query.shape
    kv_rows = keys.shape[0]
    heads = kv_rows // HD
    group = query_rows // heads
    q_spec = pl.BlockSpec((group, length), lambda h: (h, 0))
    kv_spec = pl.BlockSpec((HD, length), lambda h: (h, 0))
    q_out = jax.ShapeDtypeStruct((query_rows, length), BF)
    kv_out = jax.ShapeDtypeStruct((kv_rows, length), BF)
    return pl.pallas_call(
        functools.partial(attend_back_kernel, min(256, length)),
        grid=(heads,),
        out_shape=(q_out, kv_out, kv_out),
        in_specs=[
            whole(start),
            whole(cosine),
            whole(sine),
            q_spec,
            kv_spec,
            kv_spec,
            pl.BlockSpec((1, group // HD, length), lambda h: (h, 0, 0)),
            q_spec,
        ],
        out_specs=(q_spec, kv_spec, kv_spec),
        scratch_shapes=[pltpu.VMEM((HD, length), F32), pltpu.VMEM((HD, length), F32)],
        compiler_params=params(),
        cost_estimate=cost(6 * query_rows * length * length, query, query, grad, grad),
    )(start, cosine, sine, query, keys, values, logs, grad)


def second_grads_kernel(count, *refs):
    left0, left1, rights, out_ref = refs[0], refs[1], refs[2:-1], refs[-1]
    over_rows = (((1,), (1,)), ((), ()))
    turned = left0[...].T, left1[...].T
    at = 0
    for k, right in enumerate(rights):
        got = lax.dot_general(turned[k >= count], right[...], over_rows, preferred_element_type=F32)
        out_ref[:, at : at + got.shape[1]] = got.astype(BF)
        at += got.shape[1]


def second_grads(left0, rights0, left1, right1):
    length, depth = left0.shape
    tile = 256
    rights = [*rights0, right1]
    cols = sum(r.shape[0] for r in rights)
    out = jax.ShapeDtypeStruct((depth, cols), BF)
    left = pl.BlockSpec((length, tile), lambda i: (0, i))
    return pl.pallas_call(
        functools.partial(second_grads_kernel, len(rights0)),
        grid=(depth // tile,),
        out_shape=out,
        in_specs=[left, left] + [whole(r) for r in rights],
        out_specs=pl.BlockSpec((tile, cols), lambda i: (i, 0)),
        compiler_params=params(),
        cost_estimate=cost(2 * length * depth * cols, left0, left1, *rights, out),
    )(left0, left1, *rights)


def first_grads_kernel(left0, left1, g0, g1, g2, low, extra, out_ref):
    cols = g0.shape[1]
    turned = left0[...].T
    for k, right in enumerate((g0, g1, g2)):
        got = jnp.dot(turned, right[...], preferred_element_type=F32)
        out_ref[:, k * cols : (k + 1) * cols] = got.astype(BF)
    got = jnp.dot(left1[...].T, low[...], preferred_element_type=F32)
    out_ref[:, 3 * cols : 4 * cols] = got.astype(BF)
    out_ref[:, 4 * cols :] = extra[...]


def first_grads(left0, rights, left1, low, extra):
    length, depth = left0.shape
    tile = 256
    cols = low.shape[1]
    width = 4 * cols + extra.shape[1]
    out = jax.ShapeDtypeStruct((depth, width), BF)
    left = pl.BlockSpec((length, tile), lambda i: (0, i))
    return pl.pallas_call(
        first_grads_kernel,
        grid=(depth // tile,),
        out_shape=out,
        in_specs=[left, left]
        + [whole(r) for r in (*rights, low)]
        + [pl.BlockSpec((tile, extra.shape[1]), lambda i: (i, 0))],
        out_specs=pl.BlockSpec((tile, width), lambda i: (i, 0)),
        compiler_params=params(),
        cost_estimate=cost(8 * length * depth * cols, left0, left1, *rights, low, out),
    )(left0, left1, *rights, low, extra)


def inv_rms(values):
    return lax.rsqrt(jnp.mean(values * values, axis=-1, keepdims=True) + EPS)


def norm_low(values, gain):
    return (values * inv_rms(values) * gain).astype(BF)


def norm_back(grad_normed, values, gain, grad_out):
    q = inv_rms(values)
    grad_gain = jnp.sum(grad_normed * values * q, axis=0)
    a2 = grad_normed * gain
    inner = jnp.mean(a2 * values, axis=-1, keepdims=True)
    return grad_out + q * a2 - values * (q * q * q * inner), grad_gain


def rope_tables(positions):
    half = HD // 2
    freq = jnp.exp(jnp.arange(half, dtype=F32) * (-2.0 * math.log(THETA) / (2 * half)))
    angle = freq[:, None] * positions[None, :]
    return jnp.cos(angle), jnp.sin(angle)


def conv_mix(mixed, kernel, same_one, same_two):
    driven = mixed[0] * mixed[2]
    zero = jnp.zeros((2, driven.shape[1]), driven.dtype)
    back_one = jnp.concatenate([zero[:1], driven[:-1]], axis=0) * same_one
    back_two = jnp.concatenate([zero, driven[:-2]], axis=0) * same_two
    return mixed[1] * (kernel[0] * driven + kernel[1] * back_one + kernel[2] * back_two)


def per_device(
    tokens_in,
    segments,
    gains,
    taps,
    in_proj,
    out_proj,
    gate_up_a,
    down_a,
    query_w,
    key_value_w,
    attn_out_w,
    gate_up_b,
    down_b,
    cotangent,
):
    half = tokens_in.shape[1]
    segment_ids = segments[0]
    length = segment_ids.shape[0]
    rows = in_proj.shape[0]
    width = rows * lax.axis_size("dp")
    rank = lax.axis_index("tensor")

    def in_order(own):
        other = swap(own)
        first = jnp.where(rank == 0, own, other)
        second = jnp.where(rank == 0, other, own)
        return jnp.concatenate([first, second], axis=0)

    def own_half(full):
        return lax.dynamic_slice_in_dim(full, rank * half, half, 0)

    def other_half(full):
        return lax.dynamic_slice_in_dim(full, (1 - rank) * half, half, 0)

    def four(own):
        far = flip_x(own)
        return own, swap(own), far, swap(far)

    def far_total(far):
        return (far[0] + swap(far[1]).astype(F32)).astype(BF)

    def four_total(near, far_sum):
        return near[0] + swap(near[1]).astype(F32) + flip_x(far_sum).astype(F32)

    def four_back(near, far):
        return four_total(near, far_total(far))

    misc = jnp.concatenate(
        [gains.T, taps.T, jnp.zeros((rows, 128 - gains.shape[0] - taps.shape[0]), BF)], axis=1
    )
    conv_cols = in_proj.shape[2]
    query_cols = query_w.shape[1]
    kv_cols = key_value_w.shape[2]
    unit = down_a.shape[0] // 2

    def shared(gate_up, down):
        parts = [halves(v, 1) for v in (gate_up[:, 0], gate_up[:, 1], down.T)]
        mine = jnp.concatenate([p[0] for p in parts], axis=1)
        return by_x(mine, flip_x(jnp.concatenate([p[1] for p in parts], axis=1)), 0)

    own = jnp.concatenate([misc, in_proj[:, 0], in_proj[:, 1], in_proj[:, 2], out_proj.T], axis=1)
    conv_w = ring_gather(own)
    in_w, w_out = conv_w[:, : 128 + 3 * conv_cols], conv_w[:, 128 + 3 * conv_cols :]
    ff_a = ring_gather(shared(gate_up_a, down_a))
    own = jnp.concatenate(
        [query_w, key_value_w[:, 0], key_value_w[:, 1], attn_out_w.T], axis=1
    )
    attn_pair, ff_b_pair = by_x(own, flip_x(own), 0), shared(gate_up_b, down_b)
    attn_w = ring_gather(attn_pair)
    ff_b = ring_gather(ff_b_pair)
    sent, _, _ = lax.optimization_barrier((in_w, attn_pair, ff_b_pair))
    in_other = flip_x(sent)
    sent, in_other = lax.optimization_barrier((w_out, in_other))
    in_w = between(in_w, in_other)
    out_other = flip_x(sent)
    w_qkv = attn_w[:, : query_cols + 2 * kv_cols]
    w_attn = attn_w[:, query_cols + 2 * kv_cols :]
    w_in = [in_w[:, 128 + k * conv_cols : 128 + (k + 1) * conv_cols] for k in range(3)]
    misc_all = in_w[:, :128]

    gain_rows = misc_all[:, :4].T.astype(F32)
    taps_all = ring_order(misc_all[:, 4:7].T, 1, back=True).astype(F32)
    kernel = lax.dynamic_slice_in_dim(taps_all, rank * conv_cols, conv_cols, 1)

    index = jnp.arange(length)
    first_of_doc = jnp.sum((segment_ids[None, :] < segment_ids[:, None]).astype(jnp.int32), axis=1)
    positions = (index - first_of_doc).astype(F32)
    same_one = (positions >= 1).astype(F32)[:, None]
    same_two = (positions >= 2).astype(F32)[:, None]
    cosine, sine = rope_tables(positions)
    doc_start = first_of_doc[None, :]

    hidden_zero = ring_order(tokens_in[0], 1).astype(F32)
    first_full = in_order(norm_low(hidden_zero, gain_rows[0]))
    mixed = [dot_nn(first_full, w) for w in w_in]
    conv_out, conv_pull = jax.vjp(
        lambda mixed_in, kernel_in: conv_mix(mixed_in, kernel_in, same_one, same_two), mixed, kernel
    )
    conv_low, out_other = lax.optimization_barrier((conv_out.astype(BF), out_other))
    w_out = between(w_out, out_other)

    def collect(own, other, w):
        sent = swap(dot_nt(other, w).astype(BF))
        return dot_nt(own, w) + sent.astype(F32)

    hidden_one = hidden_zero + collect(own_half(conv_low), other_half(conv_low), w_out)

    def feed_forward(hidden, gain, weights):
        own = norm_low(hidden, gain)
        sibling, across = swap(own), flip_x(own)
        near = ff_ahead(own, sibling, weights, unit)
        near, across = lax.optimization_barrier((near, across))
        blocks = own, sibling, across, swap(across)
        far = ff_ahead(*blocks[2:], weights, unit)
        return hidden + four_back(near[2], far[2]), (blocks, near, far)

    def feed_back(grad_out, hidden, gain, weights, kept, settle, other):
        blocks, near, far = kept
        own = grad_out.astype(BF)
        sibling, across = swap(own), flip_x(own)
        near_back, near_sum = ff_back(own, sibling, weights, unit, near[0])
        inputs, near_sum = lax.optimization_barrier((other[1:], near_sum))
        other = other[0](*inputs)
        near_sum, across, settle, other = lax.optimization_barrier((near_sum, across, settle, other))
        far_in = across, swap(across)
        far_back, far_sum = ff_back(*far_in, weights, unit, far[0])
        far_sum, far_back = lax.optimization_barrier((far_total(far_sum), far_back))
        g_gate_up = weight_grad(blocks, near_back, far_back)
        upper, lower = jnp.split(far_sum, 2, axis=0)
        upper, g_gate_up = lax.optimization_barrier((flip_x(upper), g_gate_up))
        product, upper = lax.optimization_barrier((near[1], upper))
        g_down = weight_grad([own, sibling, *far_in], product, far[1], 0)
        lower, g_down = lax.optimization_barrier((flip_x(lower), g_down))
        whole_far = jnp.concatenate([upper, lower], axis=0)
        grad_normed = near_sum[0] + swap(near_sum[1]).astype(F32) + whole_far.astype(F32)
        grad_normed, g_down = lax.optimization_barrier((grad_normed, g_down))
        grad_hidden, grad_gain = norm_back(grad_normed, hidden, gain, grad_out)
        return grad_hidden, grad_gain, ring_sum(g_gate_up), g_down, settle, ring_sum(other)

    def feed_both(hidden, gain, weights, grad_out, grads):
        own = norm_low(hidden, gain)
        sibling, across = swap(own), flip_x(own)
        near, near_back, near_down, near_sum = ff_both(own, sibling, *grads[:2], weights, unit)
        near_sum, across = lax.optimization_barrier((near_sum, across))
        blocks = own, sibling, across, swap(across)
        far, far_back, far_down, far_sum = ff_both(*blocks[2:], *grads[2:], weights, unit)
        far_sum, far = lax.optimization_barrier((far_total(far_sum), far))
        g_gate_up = weight_grad(blocks, near_back, far_back)
        near, g_gate_up = lax.optimization_barrier((near, g_gate_up))
        grad_w = weight_grad(grads, near, far, 0, g_gate_up)
        grad_normed = four_total(near_sum, far_sum)
        grad_normed, grad_w = lax.optimization_barrier((grad_normed, grad_w))
        grad_hidden, grad_gain = norm_back(grad_normed, hidden, gain, grad_out)
        sums = ring_sum(grad_w)
        return grad_hidden, grad_gain, sums, near_down, far_down

    def finish_shared(summed):
        mine, theirs = halves(summed, 0)
        return mine.astype(F32), flip_x(theirs).astype(F32)

    def finish(summed):
        mine, theirs = halves(summed, 0)
        return mine.astype(F32) + flip_x(theirs).astype(F32)

    def finish_all(summed):
        mine, theirs = finish_shared(summed)
        down, gate, up = (
            by_x(mine[:, k * unit : (k + 1) * unit], theirs[:, k * unit : (k + 1) * unit], 1)
            for k in range(3)
        )
        return jnp.stack([gate, up], axis=1), down.T

    def finish_gate_up(summed):
        mine, theirs = finish_shared(summed)
        gate = by_x(mine[:, :unit], theirs[:, :unit], 1)
        up = by_x(mine[:, unit:], theirs[:, unit:], 1)
        return jnp.stack([gate, up], axis=1)

    hidden_two, kept_a = feed_forward(hidden_one, gain_rows[1], ff_a)

    def my_part(full, other=False):
        start = (1 - rank if other else rank) * half
        return lax.dynamic_slice_in_dim(full, start, half, 1)

    def from_heads(full, w):
        over = (((0,), (1,)), ((), ()))
        sent = lax.dot_general(my_part(full, True), w, over, preferred_element_type=F32).astype(BF)
        kept = lax.dot_general(my_part(full), w, over, preferred_element_type=F32)
        return kept + swap(sent).astype(F32)

    def to_heads(w, full):
        return lax.dot_general(w, full, (((0,), (1,)), ((), ())), preferred_element_type=F32)

    third_full = in_order(norm_low(hidden_two, gain_rows[2]))
    qkv = to_heads(w_qkv, third_full)
    grad_own, hidden_two = lax.optimization_barrier((ring_order(cotangent[0], 1), hidden_two))
    grad_blocks = [grad_own, swap(grad_own), flip_x(grad_own)]
    query, keys, values, attended, logs = attend(doc_start, cosine, sine, qkv, query_cols, kv_cols)
    attended, grads_across = lax.optimization_barrier((attended, grad_blocks[2]))
    grad_blocks = [*grad_blocks[:2], grads_across, swap(grads_across)]
    hidden_three = hidden_two + from_heads(attended, w_attn)

    grad_four = ring_order(cotangent[0], 1).astype(F32)
    grad_three, gain_grad_three, sum_b, near, far = feed_both(
        hidden_three, gain_rows[3], ff_b, grad_four, grad_blocks
    )
    attn_full = in_order(grad_three.astype(BF))
    far_sum = far_total(far)
    grad_attended = to_heads(w_attn, attn_full).astype(BF)
    grad_attended, near, far_sum = lax.optimization_barrier((grad_attended, near, far_sum))
    grad_qkv = attend_back(doc_start, cosine, sine, query, keys, values, logs, grad_attended)
    grad_qkv, far_sum = lax.optimization_barrier((grad_qkv, flip_x(far_sum)))
    hidden_four = hidden_three + (near[0] + swap(near[1]).astype(F32) + far_sum.astype(F32))
    output = ring_order(hidden_four.astype(BF), 1, back=True)[None]
    grad_third = from_heads(jnp.concatenate(grad_qkv, axis=0), w_qkv)
    grad_two, gain_grad_two = norm_back(grad_third, hidden_two, gain_rows[2], grad_three)

    grad_one, gain_grad_one, sum_gu_a, g_down_a, (sum_b,), sum_second = feed_back(
        grad_two,
        hidden_one,
        gain_rows[1],
        ff_a,
        kept_a,
        (sum_b,),
        (second_grads, third_full, grad_qkv, attn_full, attended),
    )
    conv_full = in_order(grad_one.astype(BF))
    conv_full, sum_second = lax.optimization_barrier((conv_full, sum_second))
    grad_conv = dot_nn(conv_full, w_out)
    grad_mixed, grad_kernel = conv_pull(grad_conv)
    grad_mixed = [g.astype(BF) for g in grad_mixed]
    grad_first_w = first_grads(first_full, grad_mixed, conv_full, conv_low, g_down_a)
    sum_conv = ring_sum(grad_first_w)
    grad_mixed, sum_gu_a, _ = lax.optimization_barrier((grad_mixed, sum_gu_a, grad_first_w))
    own_first = sum(dot_nt(own_half(g), w) for g, w in zip(grad_mixed, w_in))
    other_first = sum(dot_nt(other_half(g), w) for g, w in zip(grad_mixed, w_in))
    grad_first = own_first + swap(other_first.astype(BF)).astype(F32)
    grad_zero, gain_grad_zero = norm_back(grad_first, hidden_zero, gain_rows[0], grad_one)

    grad_input = ring_order(grad_zero, 1, back=True)[None]

    kernel_full = lax.dynamic_update_slice(
        jnp.zeros((3, width), F32), grad_kernel, (0, rank * conv_cols)
    )
    small = jnp.concatenate(
        [
            ring_order(
                jnp.stack([gain_grad_zero, gain_grad_one, gain_grad_two, gain_grad_three]), 1, back=True
            ),
            kernel_full,
            jnp.zeros((1, width), F32),
        ],
        axis=0,
    )
    step, count = 1, lax.axis_size("dp")
    small = small + swap(small)
    while step < count:
        small = small + lax.ppermute(small, "dp", [(i, i ^ step) for i in range(count)])
        step *= 2
    small_sum = lax.dynamic_slice_in_dim(small, lax.axis_index("dp") * rows, rows, 1)
    sum_b, sum_second, sum_gu_a = lax.optimization_barrier((sum_b, sum_second, sum_gu_a))
    summed_gu_b, summed_dn_b = finish_all(sum_b)
    summed_attn_w = finish(sum_second)
    summed_gu_a = finish_gate_up(sum_gu_a)
    mine, theirs = halves(sum_conv, 0)
    mine, theirs = mine.astype(F32), flip_x(theirs).astype(F32)
    summed_conv = mine[:, : 4 * conv_cols] + theirs[:, : 4 * conv_cols]
    summed_dn_a = by_x(mine[:, 4 * conv_cols :], theirs[:, 4 * conv_cols :], 1).T
    summed_qkv = summed_attn_w[:, : query_cols + 2 * kv_cols]
    summed_attn = summed_attn_w[:, query_cols + 2 * kv_cols :].T
    summed_win = summed_conv[:, : 3 * conv_cols].reshape(rows, 3, conv_cols)
    summed_wout = summed_conv[:, 3 * conv_cols :].T
    return (
        output,
        grad_input,
        small_sum[:4],
        small_sum[4:7],
        summed_win,
        summed_wout,
        summed_gu_a,
        summed_dn_a,
        summed_qkv[:, :query_cols],
        summed_qkv[:, query_cols:].reshape(rows, 2, kv_cols),
        summed_attn,
        summed_gu_b,
        summed_dn_b,
    )


def solution(mesh):
    return jax.shard_map(
        per_device,
        mesh=mesh,
        in_specs=(
            P("dp", "tensor", None),
            P("dp", None),
            P(None, "dp"),
            P(None, "dp"),
            P("dp", None, "tensor"),
            P("tensor", "dp"),
            P("dp", None, "tensor"),
            P("tensor", "dp"),
            P("dp", "tensor"),
            P("dp", None, "tensor"),
            P("tensor", "dp"),
            P("dp", None, "tensor"),
            P("tensor", "dp"),
            P("dp", "tensor", None),
        ),
        out_specs=(
            P("dp", "tensor", None),
            P("dp", "tensor", None),
            P(None, "dp"),
            P(None, "dp"),
            P("dp", None, "tensor"),
            P("tensor", "dp"),
            P("dp", None, "tensor"),
            P("tensor", "dp"),
            P("dp", "tensor"),
            P("dp", None, "tensor"),
            P("tensor", "dp"),
            P("dp", None, "tensor"),
            P("tensor", "dp"),
        ),
        check_vma=False,
    )
```
